768 devices in a mesh: rep: 192 (over z, y, core), tp: 4 (over x).
Axes of the slice: x: 4, y: 8, z: 12, core: 2. Of those that a mesh axis runs over, the one named last changes fastest.
Arguments:
- grads: bfloat16 [192, 128, 22016], P('rep', None, 'tp'), may hold values from -135 to 135
- error: bfloat16 [192, 128, 22016], P('rep', None, 'tp'), may hold values from -3 to 3
- q_prev: float32 [22016, 32], P('tp'), may hold values from -6 to 6
Outputs:
- ortho_basis: float32 [128, 32], replicated
- q_next: float32 [22016, 32], P('tp')
- error_next: bfloat16 [192, 128, 22016], P('rep', None, 'tp')
The draws below stay inside these ranges and needn't reach their ends.
All inputs are finite; a program needn't handle non-finite values.
Results may differ from the reference program's by a relative error of at most 0.001.
Values sent between devices are 32-bit elements; how exact they have to be, the bound alone decides.
A program may use at most 32 MiB of HBM per device.

```python
import jax
import jax.numpy as jnp
from jax import lax

COLS = 22016
ROWS = 128
RANK = 32
REPLICAS = 192
N_REP = 192


def draw_grads(key, part):
    key = jax.random.fold_in(key, 1)
    keys = jax.random.split(key, 3)
    replica_scale = (1.0 + 2.0 * jnp.arange(REPLICAS, dtype=jnp.float32) / max(REPLICAS - 1, 1)).reshape(REPLICAS, 1, 1)
    row_scale = jnp.exp(jax.random.uniform(keys[0], (1, ROWS, 1), jnp.float32, jnp.log(0.3), jnp.log(3.0)))
    col_scale = jnp.exp(jax.random.uniform(keys[1], (1, 1, COLS), jnp.float32, jnp.log(0.3), jnp.log(3.0)))
    base = jax.random.normal(keys[2], (REPLICAS, ROWS, COLS), jnp.float32)
    base = jnp.clip(base, -5.0, 5.0)
    return (base * replica_scale * row_scale * col_scale).astype(jnp.bfloat16)


def steps_of(key, shape, pieces, least, high):
    gain, own = 1.0, jax.random.fold_in(key, 6)
    for position, parts in pieces:
        draws = jnp.exp(jax.random.uniform(jax.random.fold_in(own, position), (parts,), jnp.float32, least / len(pieces), high / len(pieces)))
        gain = gain * jnp.repeat(draws, shape[position] // parts).reshape([-1 if axis == position else 1 for axis in range(len(shape))])
    return gain


def gaussian(own_key, dims, width, limit, shards=(), kind=jnp.bfloat16):
    result = jax.random.normal(own_key, dims, jnp.float32) * width
    if len(shards) > 0:
        result = steps_of(own_key, dims, shards, -0.22, 0.18) * result
    return jnp.clip(result, min=-limit, max=limit).astype(kind)


def setup_inputs(seed: int = 0) -> dict:
    key_list = jax.random.split(jax.random.key(seed), 4)
    return {
        "grads": draw_grads(jax.random.fold_in(key_list[3], 71), 0),
        "error": gaussian(key_list[1], (REPLICAS, ROWS, COLS), 0.5, 3.0, ((0, 192), (2, 4))),
        "q_prev": gaussian(key_list[2], (COLS, RANK), 1.0, 6.0, ((0, 4),), jnp.float32),
    }


def reference(grads, error, q_prev):
    highest = lax.Precision.HIGHEST

    def project(running, blocks):
        merged = blocks[0].astype(jnp.float32) + blocks[1].astype(jnp.float32)
        return (running + jnp.dot(merged.astype(jnp.float32), q_prev.astype(jnp.float32), precision=highest, preferred_element_type=jnp.float32), None)
    factor, unused = lax.scan(project, jnp.zeros((ROWS, RANK), jnp.float32), (grads, error))
    gram_matrix = jnp.dot(factor.T.astype(jnp.float32), factor.astype(jnp.float32), precision=highest, preferred_element_type=jnp.float32)
    cholesky_factor = jnp.linalg.cholesky(gram_matrix)
    ortho_basis = lax.linalg.triangular_solve(cholesky_factor, factor, left_side=False, lower=True, transpose_a=True)

    def backward(running, blocks):
        merged = blocks[0].astype(jnp.float32) + blocks[1].astype(jnp.float32)
        return (running + jnp.dot(merged.T.astype(jnp.float32), ortho_basis.astype(jnp.float32), precision=highest, preferred_element_type=jnp.float32), None)
    q_total, unused_two = lax.scan(backward, jnp.zeros((COLS, RANK), jnp.float32), (grads, error))
    q_next = q_total / N_REP
    approx = jnp.dot(ortho_basis.astype(jnp.float32), q_next.T.astype(jnp.float32), precision=highest, preferred_element_type=jnp.float32)

    def rebuild(blocks):
        merged = blocks[0].astype(jnp.float32) + blocks[1].astype(jnp.float32)
        return (merged - approx).astype(jnp.bfloat16)
    error_next = lax.map(rebuild, (grads, error))
    return (ortho_basis, q_next, error_next)
```

```python
import functools

import jax
import jax.numpy as jnp
from jax import lax
from jax.experimental import pallas as pl
from jax.experimental.pallas import tpu as pltpu
from jax.sharding import PartitionSpec as P

NZ, NY, NX = 12, 8, 4
ROWS, RANK = 128, 32
REPLICAS = 192
LOCAL = 5504
TILES = LOCAL // 128
ATOMS_A, ATOMS_B = 40, 48
ATOMS = ATOMS_A + ATOMS_B
REAL = 2 * TILES
CHUNKS = ((0, 11), (11, 11), (22, 11), (33, 10))
MESH = pl.DeviceIdType.MESH
F32, BF16 = jnp.float32, jnp.bfloat16


def split3(v):
    hi = v.astype(BF16)
    rest = v - hi.astype(F32)
    mid = rest.astype(BF16)
    lo = (rest - mid.astype(F32)).astype(BF16)
    return hi, mid, lo


def far_first(n):
    return sorted(range(1, n), key=lambda k: (-min(k, n - k), k))


def drain(ref, sem):
    pltpu.make_async_copy(ref, ref, sem).wait()


def dot_f32(a, b, dims):
    return lax.dot_general(a, b, (dims, ((), ())), precision=lax.Precision.HIGHEST, preferred_element_type=F32)


def inverse_factor(gram):
    row = lax.broadcasted_iota(jnp.int32, (RANK, 128), 0)
    lane = lax.broadcasted_iota(jnp.int32, (RANK, 128), 1)
    work = jnp.concatenate([gram, jnp.zeros((RANK, 128 - RANK), F32)], axis=1)
    work = work + (lane == row + RANK).astype(F32)

    def step(k, work):
        at_row = jnp.sum(jnp.where(row == k, work, 0.0), axis=0, keepdims=True)
        column = jnp.sum(jnp.where(lane == k, work, 0.0), axis=1, keepdims=True)
        pivot = jnp.sum(jnp.where(lane[:1] == k, at_row, 0.0), axis=1, keepdims=True)
        scale = 1.0 / jnp.sqrt(pivot)
        scaled = at_row * scale
        reduced = work - (column * scale) * scaled
        return jnp.where(row == k, scaled, jnp.where(row > k, reduced, work))

    return lax.fori_loop(0, RANK, step, work)[:, RANK : 2 * RANK]


def reduce_kernel(
    g_ref, e_ref, q_ref, out_ref, small,
    ge, qv, f_part, f_core, f_x, f_y, f_z, f_full,
    p_part, p_core, p_sum, a_one, b_one, a_two, b_two, fin,
    load_sem, out_sem, ssem, rsem,
):
    rep, x = lax.axis_index("rep"), lax.axis_index("tp")
    c = lax.rem(rep, 2)
    y = lax.rem(rep // 2, NY)
    z = rep // (2 * NY)

    def at(zz, yy, cc, xx):
        return {"rep": (zz * NY + yy) * 2 + cc, "tp": xx}

    def on_x(k):
        return lax.rem(x + k, NX)

    def on_y(k):
        return lax.rem(y + k, NY)

    def on_z(k):
        return lax.rem(z + k, NZ)

    other = at(z, y, 1 - c, x)
    xs = [at(z, y, c, on_x(k)) for k in far_first(NX)]
    ys = [(on_y(k), at(z, on_y(k), c, x)) for k in far_first(NY)]
    zs = [(on_z(k), at(on_z(k), y, c, x)) for k in far_first(NZ)]

    def send(src, dst, sem, device):
        pltpu.make_async_remote_copy(
            src_ref=src, dst_ref=dst, send_sem=ssem.at[sem], recv_sem=rsem.at[sem], device_id=device, device_id_type=MESH
        ).start()

    loads = []
    for i, (t0, nt) in enumerate(CHUNKS):
        cols = pl.ds(t0 * 128, nt * 128)
        group = [
            pltpu.make_async_copy(q_ref.at[:, cols], qv.at[:, cols], load_sem.at[3 * i]),
            pltpu.make_async_copy(g_ref.at[0, :, cols], ge.at[pl.ds(0, ROWS), cols], load_sem.at[3 * i + 1]),
            pltpu.make_async_copy(e_ref.at[0, :, cols], ge.at[pl.ds(ROWS, ROWS), cols], load_sem.at[3 * i + 2]),
        ]
        for copy in group:
            copy.start()
        loads.append(group)

    barrier = pltpu.get_barrier_semaphore()
    partners = [other] + xs + [d for _, d in ys] + [d for _, d in zs]
    for device in partners:
        pl.semaphore_signal(barrier, inc=1, device_id=device, device_id_type=MESH)

    both = jnp.zeros((3 * RANK, 2 * ROWS), F32)
    for (t0, nt), group in zip(CHUNKS, loads, strict=True):
        for copy in group:
            copy.wait()
        cols = pl.ds(t0 * 128, nt * 128)
        left = jnp.concatenate(split3(qv[:, cols]), axis=0)
        both += lax.dot_general(left, ge[:, cols], (((1,), (1,)), ((), ())), preferred_element_type=F32)
    both = both[:, :ROWS] + both[:, ROWS:]
    part = both[:RANK] + (both[RANK : 2 * RANK] + both[2 * RANK :])
    f_part[...] = part.reshape(4, 8, 128)
    p_part[:, pl.ds(REAL, ATOMS - REAL)] = jnp.zeros((2, ATOMS - REAL, 8, 128), F32)
    pl.semaphore_wait(barrier, len(partners))

    send(f_part.at[pl.ds(2 * (1 - c), 2)], f_core, 0, other)
    drain(f_core, rsem.at[0])
    f_x[x] = f_part[pl.ds(2 * c, 2)] + f_core[...]
    for device in xs:
        send(f_x.at[x], f_x.at[x], 1, device)
    drain(f_x.at[pl.ds(0, NX - 1)], rsem.at[1])
    f_y[y] = functools.reduce(jnp.add, [f_x[k] for k in range(NX)])
    for _, device in ys:
        send(f_y.at[y], f_y.at[y], 2, device)
    drain(f_y.at[pl.ds(0, NY - 1)], rsem.at[2])
    f_z[z] = functools.reduce(jnp.add, [f_y[k] for k in range(NY)])
    for _, device in zs:
        send(f_z.at[z], f_z.at[z], 3, device)
    drain(f_z.at[pl.ds(0, NZ - 1)], rsem.at[3])
    f_full[pl.ds(2 * c, 2)] = functools.reduce(jnp.add, [f_z[k] for k in range(NZ)])
    send(f_full.at[pl.ds(2 * c, 2)], f_full.at[pl.ds(2 * c, 2)], 4, other)
    drain(f_full.at[pl.ds(0, 2)], rsem.at[4])
    factor = f_full[...].reshape(RANK, ROWS)

    left = jnp.concatenate(split3(factor), axis=0)
    left = jnp.concatenate([left, left], axis=1)
    for i, (t0, nt) in enumerate(CHUNKS):
        three = jnp.dot(left, ge[:, pl.ds(t0 * 128, nt * 128)], preferred_element_type=F32)
        term = three[:RANK] + (three[RANK : 2 * RANK] + three[2 * RANK :])
        for t in range(nt):
            for r in range(4):
                p_part[r // 2, (r % 2) * TILES + t0 + t] = term[8 * r : 8 * r + 8, 128 * t : 128 * t + 128]
        for r in range(2):
            atoms = pl.ds(r * TILES + t0, nt)
            send(p_part.at[1 - c, atoms], p_core.at[atoms], 5 + i, other)
    p_core[pl.ds(REAL, ATOMS - REAL)] = jnp.zeros((ATOMS - REAL, 8, 128), F32)
    for i, (t0, nt) in enumerate(CHUNKS):
        drain(p_core.at[pl.ds(0, 2 * nt)], rsem.at[5 + i])
    p_sum[...] = p_part[c] + p_core[...]

    na, nb = ATOMS_A // NY, ATOMS_B // NZ
    for yy, device in ys:
        send(p_sum.at[pl.ds(na * yy, na)], a_one.at[y], 9, device)
    for zz, device in zs:
        send(p_sum.at[pl.ds(ATOMS_A + nb * zz, nb)], b_one.at[z], 10, device)
    a_one[y] = p_sum[pl.ds(na * y, na)]
    b_one[z] = p_sum[pl.ds(ATOMS_A + nb * z, nb)]

    inverse = inverse_factor(dot_f32(factor, factor, ((1,), (1,))))
    ortho = dot_f32(inverse, factor, ((1,), (0,)))
    small[0] = ortho
    small[1] = jnp.concatenate([inverse, jnp.zeros((RANK, 128 - RANK), F32)], axis=1)

    drain(a_one.at[pl.ds(0, NY - 1)], rsem.at[9])
    a_two[z] = functools.reduce(jnp.add, [a_one[k] for k in range(NY)])
    for _, device in zs:
        send(a_two.at[z], a_two.at[z], 11, device)
    drain(b_one.at[pl.ds(0, NZ - 1)], rsem.at[10])
    b_two[y] = functools.reduce(jnp.add, [b_one[k] for k in range(NZ)])
    for _, device in ys:
        send(b_two.at[y], b_two.at[y], 12, device)

    drain(b_two.at[pl.ds(0, NY - 1)], rsem.at[12])
    own = pl.ds(ATOMS_A + nb * z, nb)
    fin[c, own] = functools.reduce(jnp.add, [b_two[k] for k in range(NY)])
    for _, device in zs:
        send(fin.at[c, own], fin.at[c, own], 14, device)
    drain(a_two.at[pl.ds(0, NZ - 1)], rsem.at[11])
    own = pl.ds(na * y, na)
    fin[c, own] = functools.reduce(jnp.add, [a_two[k] for k in range(NZ)])
    for _, device in ys:
        send(fin.at[c, own], fin.at[c, own], 13, device)

    part_a, part_b = pl.ds(0, ATOMS_A), pl.ds(ATOMS_A, ATOMS_B)
    drain(fin.at[c, pl.ds(0, ATOMS_A - na)], rsem.at[13])
    send(fin.at[c, part_a], fin.at[c, part_a], 15, other)
    drain(fin.at[c, pl.ds(0, ATOMS_B - nb)], rsem.at[14])
    send(fin.at[c, part_b], fin.at[c, part_b], 16, other)
    drain(fin.at[c, part_a], rsem.at[15])
    drain(fin.at[c, part_b], rsem.at[16])
    out = pltpu.make_async_copy(fin, out_ref, out_sem.at[0])
    out.start()

    drain(f_core, ssem.at[0])
    drain(f_x.at[pl.ds(0, NX - 1)], ssem.at[1])
    drain(f_y.at[pl.ds(0, NY - 1)], ssem.at[2])
    drain(f_z.at[pl.ds(0, NZ - 1)], ssem.at[3])
    drain(f_full.at[pl.ds(0, 2)], ssem.at[4])
    for i, (_, nt) in enumerate(CHUNKS):
        drain(p_core.at[pl.ds(0, 2 * nt)], ssem.at[5 + i])
    drain(a_one.at[pl.ds(0, NY - 1)], ssem.at[9])
    drain(b_one.at[pl.ds(0, NZ - 1)], ssem.at[10])
    drain(a_two.at[pl.ds(0, NZ - 1)], ssem.at[11])
    drain(b_two.at[pl.ds(0, NY - 1)], ssem.at[12])
    drain(fin.at[c, pl.ds(0, ATOMS_A - na)], ssem.at[13])
    drain(fin.at[c, pl.ds(0, ATOMS_B - nb)], ssem.at[14])
    drain(fin.at[c, part_a], ssem.at[15])
    drain(fin.at[c, part_b], ssem.at[16])
    out.wait()


def apply_kernel(g_ref, e_ref, p_ref, small, ortho_ref, q_ref, error_ref, gv, ev, pv, qv, err, load_sem, out_sem):
    whole = pltpu.make_async_copy(p_ref, pv, load_sem.at[2 * len(CHUNKS)])
    whole.start()
    loads = []
    for i, (t0, nt) in enumerate(CHUNKS):
        cols = pl.ds(t0 * 128, nt * 128)
        group = [
            pltpu.make_async_copy(g_ref.at[0, :, cols], gv.at[:, cols], load_sem.at[2 * i]),
            pltpu.make_async_copy(e_ref.at[0, :, cols], ev.at[:, cols], load_sem.at[2 * i + 1]),
        ]
        for copy in group:
            copy.start()
        loads.append(group)
    ortho_t = small[0]
    ortho_ref[...] = ortho_t
    first = stack_left(small[1][:, :RANK])
    second = stack_left(jnp.swapaxes(ortho_t, 0, 1))
    whole.wait()
    outs = []
    for i, (t0, nt) in enumerate(CHUNKS):
        cols = pl.ds(t0 * 128, nt * 128)
        total = jnp.concatenate(
            [jnp.concatenate([pv[r // 2, (r % 2) * TILES + t0 + t] for t in range(nt)], axis=1) for r in range(4)], axis=0
        )
        q_next = jnp.dot(first, stack_right(total), preferred_element_type=F32) / REPLICAS
        qv[:, cols] = q_next
        outs.append(pltpu.make_async_copy(qv.at[:, cols], q_ref.at[:, cols], out_sem.at[2 * i]))
        outs[-1].start()
        approx = jnp.dot(second, stack_right(q_next), preferred_element_type=F32)
        for copy in loads[i]:
            copy.wait()
        merged = gv[:, cols].astype(F32) + ev[:, cols].astype(F32)
        err[:, cols] = (merged - approx).astype(BF16)
        outs.append(pltpu.make_async_copy(err.at[:, cols], error_ref.at[0, :, cols], out_sem.at[2 * i + 1]))
        outs[-1].start()
    for copy in outs:
        copy.wait()


def stack_left(v):
    hi, mid, lo = split3(v)
    return jnp.concatenate([hi, hi, hi, mid, mid, lo], axis=1)


def stack_right(v):
    hi, mid, lo = split3(v)
    return jnp.concatenate([hi, mid, lo, hi, mid, hi], axis=0)


def shards(grads, error, q_prev):
    na, nb = ATOMS_A // NY, ATOMS_B // NZ
    n_chunks = len(CHUNKS)
    vmem, anywhere = pl.BlockSpec(memory_space=pltpu.VMEM), pl.BlockSpec(memory_space=pl.ANY)

    def atoms(*lead):
        return pltpu.VMEM((*lead, 8, 128), F32)

    total, small = pl.pallas_call(
        reduce_kernel,
        out_shape=(jax.ShapeDtypeStruct((2, ATOMS, 8, 128), F32), jax.ShapeDtypeStruct((2, RANK, 128), F32)),
        in_specs=[anywhere] * 3,
        out_specs=(anywhere, vmem),
        scratch_shapes=[
            pltpu.VMEM((2 * ROWS, LOCAL), BF16),
            pltpu.VMEM((RANK, LOCAL), F32),
            atoms(4), atoms(2), atoms(NX, 2), atoms(NY, 2), atoms(NZ, 2), atoms(4),
            atoms(2, ATOMS), atoms(ATOMS), atoms(ATOMS),
            atoms(NY, na), atoms(NZ, nb), atoms(NZ, na), atoms(NY, nb), atoms(2, ATOMS),
            pltpu.SemaphoreType.DMA((3 * n_chunks,)),
            pltpu.SemaphoreType.DMA((1,)),
            pltpu.SemaphoreType.DMA((17,)),
            pltpu.SemaphoreType.DMA((17,)),
        ],
        compiler_params=pltpu.CompilerParams(collective_id=0, has_side_effects=True, vmem_limit_bytes=20 * 2**20),
        name="reduce_factors",
    )(grads, error, jnp.swapaxes(q_prev, 0, 1))
    ortho_t, q_t, error_next = pl.pallas_call(
        apply_kernel,
        out_shape=(
            jax.ShapeDtypeStruct((RANK, ROWS), F32),
            jax.ShapeDtypeStruct((RANK, LOCAL), F32),
            jax.ShapeDtypeStruct((1, ROWS, LOCAL), BF16),
        ),
        in_specs=[anywhere] * 3 + [vmem],
        out_specs=(vmem, anywhere, anywhere),
        scratch_shapes=[
            pltpu.VMEM((ROWS, LOCAL), BF16),
            pltpu.VMEM((ROWS, LOCAL), BF16),
            atoms(2, ATOMS),
            pltpu.VMEM((RANK, LOCAL), F32),
            pltpu.VMEM((ROWS, LOCAL), BF16),
            pltpu.SemaphoreType.DMA((2 * n_chunks + 1,)),
            pltpu.SemaphoreType.DMA((2 * n_chunks,)),
        ],
        compiler_params=pltpu.CompilerParams(vmem_limit_bytes=20 * 2**20),
        name="apply_factors",
    )(grads, error, total, small)
    return jnp.swapaxes(ortho_t, 0, 1), jnp.swapaxes(q_t, 0, 1), error_next


def solution(mesh):
    in_specs = (P("rep", None, "tp"), P("rep", None, "tp"), P("tp", None))
    out_specs = (P(), P("tp", None), P("rep", None, "tp"))
    return jax.shard_map(shards, mesh=mesh, in_specs=in_specs, out_specs=out_specs, check_vma=False)
```

```python
import functools

import jax
import jax.numpy as jnp
from jax import lax
from jax.experimental import pallas as pl
from jax.experimental.pallas import tpu as pltpu
from jax.sharding import PartitionSpec as P

NZ, NY, NX = 12, 8, 4
ROWS, RANK = 128, 32
REPLICAS = 192
LOCAL = 5504
TILES = LOCAL // 128
ATOMS_A, ATOMS_B = 40, 48
TILES_B = 23
ATOMS = ATOMS_A + ATOMS_B
CHUNKS = ((0, 12), (12, 11), (23, 10), (33, 10))
MESH = pl.DeviceIdType.MESH
F32, BF16 = jnp.float32, jnp.bfloat16


def split3(v):
    hi = v.astype(BF16)
    rest = v - hi.astype(F32)
    mid = rest.astype(BF16)
    lo = (rest - mid.astype(F32)).astype(BF16)
    return hi, mid, lo


def atom_of(tile):
    return 2 * tile if tile < TILES_B else ATOMS_B + 2 * (tile - TILES_B)


def far_first(n):
    return sorted(range(1, n), key=lambda k: (-min(k, n - k), k))


def drain(ref, sem):
    pltpu.make_async_copy(ref, ref, sem).wait()


def dot_f32(a, b, dims):
    return lax.dot_general(a, b, (dims, ((), ())), precision=lax.Precision.HIGHEST, preferred_element_type=F32)


def inverse_factor(gram):
    row = lax.broadcasted_iota(jnp.int32, (RANK, 128), 0)
    lane = lax.broadcasted_iota(jnp.int32, (RANK, 128), 1)
    work = jnp.concatenate([gram, jnp.zeros((RANK, 128 - RANK), F32)], axis=1)
    work = work + (lane == row + RANK).astype(F32)

    def step(k, work):
        column = jnp.sum(jnp.where(lane == k, work, 0.0), axis=1, keepdims=True)
        at_row = jnp.sum(jnp.where(row == k, work, 0.0), axis=0, keepdims=True)
        pivot = jnp.sum(jnp.where(row[:, :1] == k, column, 0.0), axis=0, keepdims=True)
        scale = lax.rsqrt(pivot)
        scale = scale * (1.5 - 0.5 * (pivot * scale) * scale)
        scaled = at_row * scale
        reduced = work - jnp.where(row[:, :1] > k, column * scale, 0.0) * scaled
        return jnp.where(row == k, scaled, reduced)

    return lax.fori_loop(0, RANK, step, work)[:, RANK : 2 * RANK]


def reduce_kernel(
    until, g_ref, e_ref, q_ref, ge, fin, small,
    qv, f_part, f_cx, f_y, f_z, f_full, p_part, p_core, p_sum, a_one, b_one, a_sum, a_two, b_two,
    load_sem, ssem, rsem,
):
    rep, x = lax.axis_index("rep"), lax.axis_index("tp")
    c = lax.rem(rep, 2)
    y = lax.rem(rep // 2, NY)
    z = rep // (2 * NY)
    na, nb = ATOMS_A // NY, ATOMS_B // NZ

    def at(zz, yy, cc, xx):
        return {"rep": (zz * NY + yy) * 2 + cc, "tp": xx}

    other = at(z, y, 1 - c, x)
    xs = [(k, lax.rem(x + k, NX)) for k in far_first(NX)]
    cxs = [(lax.rem(c + flip, 2), at(z, y, lax.rem(c + flip, 2), xx)) for flip in (1, 0) for _, xx in xs]
    cxs.append((1 - c, other))
    ys = [(yy, at(z, yy, c, x)) for yy in [lax.rem(y + k, NY) for k in far_first(NY)]]
    zs = [(zz, at(zz, y, c, x)) for zz in [lax.rem(z + k, NZ) for k in far_first(NZ)]]
    sent = []

    def send(src, dst, sem, device):
        pltpu.make_async_remote_copy(
            src_ref=src, dst_ref=dst, send_sem=ssem.at[sem], recv_sem=rsem.at[sem], device_id=device, device_id_type=MESH
        ).start()

    def arrive(ref, sem):
        drain(ref, rsem.at[sem])
        sent.append((ref, sem))

    def finish():
        for ref, sem in sent:
            drain(ref, ssem.at[sem])

    loads = []
    for i, (t0, nt) in enumerate(CHUNKS):
        cols = pl.ds(t0 * 128, nt * 128)
        group = [
            pltpu.make_async_copy(q_ref.at[:, cols], qv.at[:, cols], load_sem.at[3 * i]),
            pltpu.make_async_copy(g_ref.at[0, :, cols], ge.at[pl.ds(0, ROWS), cols], load_sem.at[3 * i + 1]),
            pltpu.make_async_copy(e_ref.at[0, :, cols], ge.at[pl.ds(ROWS, ROWS), cols], load_sem.at[3 * i + 2]),
        ]
        for copy in group:
            copy.start()
        loads.append(group)

    barrier = pltpu.get_barrier_semaphore()
    partners = [d for _, d in cxs] + [d for _, d in ys] + [d for _, d in zs]
    for device in partners:
        pl.semaphore_signal(barrier, inc=1, device_id=device, device_id_type=MESH)

    both = jnp.zeros((3 * RANK, 2 * ROWS), F32)
    for (t0, nt), group in zip(CHUNKS, loads, strict=True):
        for copy in group:
            copy.wait()
        cols = pl.ds(t0 * 128, nt * 128)
        left = jnp.concatenate(split3(qv[:, cols]), axis=0)
        both += lax.dot_general(left, ge[:, cols], (((1,), (1,)), ((), ())), preferred_element_type=F32)
    both = both[:, :ROWS] + both[:, ROWS:]
    part = both[:RANK] + (both[RANK : 2 * RANK] + both[2 * RANK :])
    f_part[...] = part.reshape(4, 8, 128)
    pad = pl.ds(2 * TILES_B, ATOMS_B - 2 * TILES_B)
    p_sum[pad] = jnp.zeros((ATOMS_B - 2 * TILES_B, 8, 128), F32)
    pl.semaphore_wait(barrier, len(partners))
    if until == 0:
        return finish()

    own = 2 * x + c
    for cc, device in cxs:
        send(f_part.at[pl.ds(2 * cc, 2)], f_cx.at[own], 0, device)
    f_cx[own] = f_part[pl.ds(2 * c, 2)]
    arrive(f_cx.at[pl.ds(0, 2 * NX - 1)], 0)
    if until == 1:
        return finish()
    f_y[y] = functools.reduce(jnp.add, [f_cx[k] for k in range(2 * NX)])
    for _, device in ys:
        send(f_y.at[y], f_y.at[y], 1, device)
    arrive(f_y.at[pl.ds(0, NY - 1)], 1)
    if until == 2:
        return finish()
    f_z[z] = functools.reduce(jnp.add, [f_y[k] for k in range(NY)])
    for _, device in zs:
        send(f_z.at[z], f_z.at[z], 2, device)
    arrive(f_z.at[pl.ds(0, NZ - 1)], 2)
    if until == 3:
        return finish()
    half = pl.ds(2 * c, 2)
    f_full[half] = functools.reduce(jnp.add, [f_z[k] for k in range(NZ)])
    send(f_full.at[half], f_full.at[half], 3, other)
    arrive(f_full.at[pl.ds(0, 2)], 3)
    factor = f_full[...].reshape(RANK, ROWS)
    if until == 4:
        return finish()

    left = jnp.concatenate(split3(factor), axis=0)
    left = jnp.concatenate([left, left], axis=1)

    def project(i):
        t0, nt = CHUNKS[i]
        three = jnp.dot(left, ge[:, pl.ds(t0 * 128, nt * 128)], preferred_element_type=F32)
        term = three[:RANK] + (three[RANK : 2 * RANK] + three[2 * RANK :])
        for t in range(nt):
            for r in range(4):
                p_part[r // 2, atom_of(t0 + t) + r % 2] = term[8 * r : 8 * r + 8, 128 * t : 128 * t + 128]
        atoms = pl.ds(atom_of(t0), 2 * nt)
        send(p_part.at[1 - c, atoms], p_core.at[atoms], 4 + i, other)

    def add_core(i):
        t0, nt = CHUNKS[i]
        atoms = pl.ds(atom_of(t0), 2 * nt)
        arrive(p_core.at[atoms], 4 + i)
        p_sum[atoms] = p_part[c, atoms] + p_core[atoms]

    project(0)
    project(1)
    project(2)
    add_core(0)
    add_core(1)
    for zz, device in zs:
        send(p_sum.at[pl.ds(nb * zz, nb)], b_one.at[z], 8, device)
    b_one[z] = p_sum[pl.ds(nb * z, nb)]
    project(3)
    add_core(2)
    add_core(3)
    for yy, device in ys:
        send(p_sum.at[pl.ds(ATOMS_B + na * yy, na)], a_one.at[y], 9, device)
    a_one[y] = p_sum[pl.ds(ATOMS_B + na * y, na)]

    if until != 6:
        inverse = inverse_factor(dot_f32(factor, factor, ((1,), (1,))))
        small[0] = dot_f32(inverse, factor, ((1,), (0,)))
        small[1] = jnp.concatenate([inverse, jnp.zeros((RANK, 128 - RANK), F32)], axis=1)
    owners = [NZ * j // na for j in range(na)]
    owned = [z == zz for zz in owners]
    is_owner = functools.reduce(jnp.logical_or, owned)
    arrive(a_one.at[pl.ds(0, NY - 1)], 9)
    if until == 5 or until == 6:
        arrive(b_one.at[pl.ds(0, NZ - 1)], 8)
        return finish()
    a_sum[...] = functools.reduce(jnp.add, [a_one[k] for k in range(NY)])
    for j, zz in enumerate(owners):

        @pl.when(z != zz)
        def _(j=j, zz=zz):
            send(a_sum.at[j], a_two.at[z], 10, at(zz, y, c, x))

        @pl.when(z == zz)
        def _(j=j):
            a_two[z] = a_sum[j]

    arrive(b_one.at[pl.ds(0, NZ - 1)], 8)
    b_two[y] = functools.reduce(jnp.add, [b_one[k] for k in range(NZ)])
    for _, device in ys:
        send(b_two.at[y], b_two.at[y], 11, device)

    for j in range(na):

        @pl.when(owned[j])
        def _(j=j):
            drain(a_two.at[pl.ds(0, NZ - 1)], rsem.at[10])
            mine = ATOMS_B + na * y + j
            fin[c, mine] = functools.reduce(jnp.add, [a_two[k] for k in range(NZ)])
            for _, device in zs:
                send(fin.at[c, mine], fin.at[c, mine], 12, device)

    arrive(b_two.at[pl.ds(0, NY - 1)], 11)
    own_b = pl.ds(nb * z, nb)
    fin[c, own_b] = functools.reduce(jnp.add, [b_two[k] for k in range(NY)])
    for _, device in zs:
        send(fin.at[c, own_b], fin.at[c, own_b], 13, device)

    @pl.when(is_owner)
    def _():
        drain(a_sum.at[pl.ds(0, na - 1)], rsem.at[12])

    @pl.when(jnp.logical_not(is_owner))
    def _():
        drain(a_sum, rsem.at[12])

    own_a = pl.ds(ATOMS_B + na * y, na)
    for _, device in ys:
        send(fin.at[c, own_a], fin.at[c, own_a], 14, device)

    part_a, part_b = pl.ds(ATOMS_B, ATOMS_A), pl.ds(0, ATOMS_B)
    arrive(fin.at[c, pl.ds(0, ATOMS_A - na)], 14)
    send(fin.at[c, part_a], fin.at[c, part_a], 15, other)
    arrive(fin.at[c, pl.ds(0, ATOMS_B - nb)], 13)
    send(fin.at[c, part_b], fin.at[c, part_b], 16, other)
    arrive(fin.at[c, part_a], 15)
    arrive(fin.at[c, part_b], 16)

    @pl.when(is_owner)
    def _():
        drain(a_sum.at[pl.ds(0, na - 1)], ssem.at[10])
        drain(a_two.at[pl.ds(0, NZ - 1)], ssem.at[12])

    @pl.when(jnp.logical_not(is_owner))
    def _():
        drain(a_sum, ssem.at[10])

    finish()


def apply_kernel(ge, total, small, ortho_ref, q_ref, error_ref, qv, err, out_sem):
    ortho_t = small[0]
    ortho_ref[...] = ortho_t
    first = stack_left(small[1][:, :RANK])
    second = stack_left(jnp.swapaxes(ortho_t, 0, 1))
    outs = []
    for i, (t0, nt) in enumerate(CHUNKS):
        cols = pl.ds(t0 * 128, nt * 128)
        rows = [jnp.concatenate([total[r // 2, atom_of(t0 + t) + r % 2] for t in range(nt)], axis=1) for r in range(4)]
        q_next = jnp.dot(first, stack_right(jnp.concatenate(rows, axis=0)), preferred_element_type=F32) / REPLICAS
        qv[:, cols] = q_next
        outs.append(pltpu.make_async_copy(qv.at[:, cols], q_ref.at[:, cols], out_sem.at[2 * i]))
        outs[-1].start()
        approx = jnp.dot(second, stack_right(q_next), preferred_element_type=F32)
        merged = ge[pl.ds(0, ROWS), cols].astype(F32) + ge[pl.ds(ROWS, ROWS), cols].astype(F32)
        err[:, cols] = (merged - approx).astype(BF16)
        outs.append(pltpu.make_async_copy(err.at[:, cols], error_ref.at[0, :, cols], out_sem.at[2 * i + 1]))
        outs[-1].start()
    for copy in outs:
        copy.wait()


def stack_left(v):
    hi, mid, lo = split3(v)
    return jnp.concatenate([hi, hi, hi, mid, mid, lo], axis=1)


def stack_right(v):
    hi, mid, lo = split3(v)
    return jnp.concatenate([hi, mid, lo, hi, mid, hi], axis=0)


def atoms(*lead):
    return pltpu.VMEM((*lead, 8, 128), F32)


VMEM, HBM = pl.BlockSpec(memory_space=pltpu.VMEM), pl.BlockSpec(memory_space=pltpu.HBM)


def reduce_all(grads, error, q_t, until=None, collective_id=0, name="reduce_factors"):
    na, nb = ATOMS_A // NY, ATOMS_B // NZ
    return pl.pallas_call(
        functools.partial(reduce_kernel, until),
        out_shape=(
            jax.ShapeDtypeStruct((2 * ROWS, LOCAL), BF16),
            jax.ShapeDtypeStruct((2, ATOMS, 8, 128), F32),
            jax.ShapeDtypeStruct((2, RANK, 128), F32),
        ),
        in_specs=[HBM] * 3,
        out_specs=(VMEM, VMEM, VMEM),
        scratch_shapes=[
            pltpu.VMEM((RANK, LOCAL), F32),
            atoms(4), atoms(2 * NX, 2), atoms(NY, 2), atoms(NZ, 2), atoms(4),
            atoms(2, ATOMS), atoms(ATOMS), atoms(ATOMS),
            atoms(NY, na), atoms(NZ, nb), atoms(na), atoms(NZ), atoms(NY, nb),
            pltpu.SemaphoreType.DMA((3 * len(CHUNKS),)),
            pltpu.SemaphoreType.DMA((17,)),
            pltpu.SemaphoreType.DMA((17,)),
        ],
        compiler_params=pltpu.CompilerParams(collective_id=collective_id, has_side_effects=True, vmem_limit_bytes=20 * 2**20),
        name=name,
    )(*[pltpu.with_memory_space_constraint(v, pltpu.HBM) for v in (grads, error, q_t)])


def apply_all(ge, total, small):
    return pl.pallas_call(
        apply_kernel,
        out_shape=(
            jax.ShapeDtypeStruct((RANK, ROWS), F32),
            jax.ShapeDtypeStruct((RANK, LOCAL), F32),
            jax.ShapeDtypeStruct((1, ROWS, LOCAL), BF16),
        ),
        in_specs=[VMEM] * 3,
        out_specs=(VMEM, HBM, HBM),
        scratch_shapes=[
            pltpu.VMEM((RANK, LOCAL), F32),
            pltpu.VMEM((ROWS, LOCAL), BF16),
            pltpu.SemaphoreType.DMA((2 * len(CHUNKS),)),
        ],
        compiler_params=pltpu.CompilerParams(vmem_limit_bytes=20 * 2**20),
        name="apply_factors",
    )(ge, total, small)


def shards(grads, error, q_prev):
    ortho_t, q_t, error_next = apply_all(*reduce_all(grads, error, jnp.swapaxes(q_prev, 0, 1)))
    return jnp.swapaxes(ortho_t, 0, 1), jnp.swapaxes(q_t, 0, 1), error_next


def solution(mesh):
    in_specs = (P("rep", None, "tp"), P("rep", None, "tp"), P("tp", None))
    out_specs = (P(), P("tp", None), P("rep", None, "tp"))
    return jax.shard_map(shards, mesh=mesh, in_specs=in_specs, out_specs=out_specs, check_vma=False)
```

```python
import functools

import jax
import jax.numpy as jnp
from jax import lax
from jax.experimental import pallas as pl
from jax.experimental.pallas import tpu as pltpu
from jax.sharding import PartitionSpec as P

NZ, NY, NX = 12, 8, 4
ROWS, RANK = 128, 32
REPLICAS = 192
LOCAL = 5504
TILES = LOCAL // 128
ATOMS_A, ATOMS_B = 40, 48
TILES_B = 23
ATOMS = ATOMS_A + ATOMS_B
CHUNKS = ((0, 12), (12, 11), (23, 10), (33, 10))
MESH = pl.DeviceIdType.MESH
F32, BF16 = jnp.float32, jnp.bfloat16


def split3(v):
    hi = v.astype(BF16)
    rest = v - hi.astype(F32)
    mid = rest.astype(BF16)
    lo = (rest - mid.astype(F32)).astype(BF16)
    return hi, mid, lo


def atom_of(tile):
    return 2 * tile if tile < TILES_B else ATOMS_B + 2 * (tile - TILES_B)


def far_first(n):
    return sorted(range(1, n), key=lambda k: (-min(k, n - k), k))


def drain(ref, sem):
    pltpu.make_async_copy(ref, ref, sem).wait()


def dot_f32(a, b, dims):
    return lax.dot_general(a, b, (dims, ((), ())), precision=lax.Precision.HIGHEST, preferred_element_type=F32)


def inverse_factor(gram):
    row = lax.broadcasted_iota(jnp.int32, (RANK, 128), 0)
    lane = lax.broadcasted_iota(jnp.int32, (RANK, 128), 1)
    work = jnp.concatenate([gram, jnp.zeros((RANK, 128 - RANK), F32)], axis=1)
    work = work + (lane == row + RANK).astype(F32)

    def step(k, work):
        column = jnp.sum(jnp.where(lane == k, work, 0.0), axis=1, keepdims=True)
        at_row = jnp.sum(jnp.where(row == k, work, 0.0), axis=0, keepdims=True)
        pivot = jnp.sum(jnp.where(row[:, :1] == k, column, 0.0), axis=0, keepdims=True)
        scale = lax.rsqrt(pivot)
        scale = scale * (1.5 - 0.5 * (pivot * scale) * scale)
        scaled = at_row * scale
        reduced = work - jnp.where(row[:, :1] > k, column * scale, 0.0) * scaled
        return jnp.where(row == k, scaled, reduced)

    return lax.fori_loop(0, RANK, step, work)[:, RANK : 2 * RANK]


def reduce_kernel(
    until, g_ref, e_ref, q_ref, ge, fin, small,
    qv, f_part, f_cx, f_y, f_z, f_full, m_own, m_other, pair, p_sum, a_one, b_one, a_sum, a_two, b_two,
    load_sem, ssem, rsem,
):
    rep, x = lax.axis_index("rep"), lax.axis_index("tp")
    c = lax.rem(rep, 2)
    y = lax.rem(rep // 2, NY)
    z = rep // (2 * NY)
    na, nb = ATOMS_A // NY, ATOMS_B // NZ

    def at(zz, yy, cc, xx):
        return {"rep": (zz * NY + yy) * 2 + cc, "tp": xx}

    other = at(z, y, 1 - c, x)
    xs = [(k, lax.rem(x + k, NX)) for k in far_first(NX)]
    cxs = [(lax.rem(c + flip, 2), at(z, y, lax.rem(c + flip, 2), xx)) for flip in (1, 0) for _, xx in xs]
    cxs.append((1 - c, other))
    ys = [(yy, at(z, yy, c, x)) for yy in [lax.rem(y + k, NY) for k in far_first(NY)]]
    zs = [(zz, at(zz, y, c, x)) for zz in [lax.rem(z + k, NZ) for k in far_first(NZ)]]
    sent = []

    def send(src, dst, sem, device):
        pltpu.make_async_remote_copy(
            src_ref=src, dst_ref=dst, send_sem=ssem.at[sem], recv_sem=rsem.at[sem], device_id=device, device_id_type=MESH
        ).start()

    def arrive(ref, sem):
        drain(ref, rsem.at[sem])
        sent.append((ref, sem))

    def finish():
        for ref, sem in sent:
            drain(ref, ssem.at[sem])

    loads = []
    for i, (t0, nt) in enumerate(CHUNKS):
        cols = pl.ds(t0 * 128, nt * 128)
        group = [
            pltpu.make_async_copy(q_ref.at[:, cols], qv.at[:, cols], load_sem.at[3 * i]),
            pltpu.make_async_copy(g_ref.at[0, :, cols], ge.at[pl.ds(0, ROWS), cols], load_sem.at[3 * i + 1]),
            pltpu.make_async_copy(e_ref.at[0, :, cols], ge.at[pl.ds(ROWS, ROWS), cols], load_sem.at[3 * i + 2]),
        ]
        for copy in group:
            copy.start()
        loads.append(group)

    barrier = pltpu.get_barrier_semaphore()
    partners = [d for _, d in cxs] + [d for _, d in ys] + [d for _, d in zs]
    for device in partners:
        pl.semaphore_signal(barrier, inc=1, device_id=device, device_id_type=MESH)

    both = jnp.zeros((3 * RANK, 2 * ROWS), F32)
    for (t0, nt), group in zip(CHUNKS, loads, strict=True):
        for copy in group:
            copy.wait()
        cols = pl.ds(t0 * 128, nt * 128)
        left = jnp.concatenate(split3(qv[:, cols]), axis=0)
        both += lax.dot_general(left, ge[:, cols], (((1,), (1,)), ((), ())), preferred_element_type=F32)
    both = both[:, :ROWS] + both[:, ROWS:]
    part = both[:RANK] + (both[RANK : 2 * RANK] + both[2 * RANK :])
    f_part[...] = part.reshape(4, 8, 128)
    pad = pl.ds(2 * TILES_B, ATOMS_B - 2 * TILES_B)
    p_sum[pad] = jnp.zeros((ATOMS_B - 2 * TILES_B, 8, 128), F32)
    pl.semaphore_wait(barrier, len(partners))
    if until == 0:
        return finish()

    own = 2 * x + c
    for cc, device in cxs:
        send(f_part.at[pl.ds(2 * cc, 2)], f_cx.at[own], 0, device)
    f_cx[own] = f_part[pl.ds(2 * c, 2)]
    for i, (t0, nt) in enumerate(CHUNKS):
        cols = pl.ds(t0 * 128, nt * 128)
        m_own[:, cols] = ge[pl.ds(0, ROWS), cols].astype(F32) + ge[pl.ds(ROWS, ROWS), cols].astype(F32)
        send(m_own.at[:, cols], m_other.at[:, cols], 4 + i, other)
    arrive(f_cx.at[pl.ds(0, 2 * NX - 1)], 0)
    if until == 1:
        return finish()
    f_y[y] = functools.reduce(jnp.add, [f_cx[k] for k in range(2 * NX)])
    for _, device in ys:
        send(f_y.at[y], f_y.at[y], 1, device)
    arrive(f_y.at[pl.ds(0, NY - 1)], 1)
    if until == 2:
        return finish()
    f_z[z] = functools.reduce(jnp.add, [f_y[k] for k in range(NY)])
    for _, device in zs:
        send(f_z.at[z], f_z.at[z], 2, device)
    for i, (t0, nt) in enumerate(CHUNKS):
        cols = pl.ds(t0 * 128, nt * 128)
        arrive(m_other.at[:, cols], 4 + i)
        for k, piece in enumerate(split3(m_own[:, cols] + m_other[:, cols])):
            pair[pl.ds(ROWS * k, ROWS), cols] = piece
    arrive(f_z.at[pl.ds(0, NZ - 1)], 2)
    if until == 3:
        return finish()
    half = pl.ds(2 * c, 2)
    f_full[half] = functools.reduce(jnp.add, [f_z[k] for k in range(NZ)])
    send(f_full.at[half], f_full.at[half], 3, other)
    if until == 4:
        arrive(f_full.at[pl.ds(0, 2)], 3)
        return finish()

    left = jnp.concatenate(split3(f_full[half].reshape(RANK // 2, ROWS)), axis=0)
    left = jnp.concatenate([left, left, left], axis=1)

    def project(i):
        t0, nt = CHUNKS[i]
        three = jnp.dot(left, pair[:, pl.ds(t0 * 128, nt * 128)], preferred_element_type=F32)
        term = three[:16] + (three[16:32] + three[32:])
        for t in range(nt):
            for r in range(2):
                p_sum[atom_of(t0 + t) + r] = term[8 * r : 8 * r + 8, 128 * t : 128 * t + 128]

    project(0)
    project(1)
    for zz, device in zs:
        send(p_sum.at[pl.ds(nb * zz, nb)], b_one.at[z], 8, device)
    b_one[z] = p_sum[pl.ds(nb * z, nb)]
    project(2)
    project(3)
    for yy, device in ys:
        send(p_sum.at[pl.ds(ATOMS_B + na * yy, na)], a_one.at[y], 9, device)
    a_one[y] = p_sum[pl.ds(ATOMS_B + na * y, na)]

    arrive(f_full.at[pl.ds(0, 2)], 3)
    factor = f_full[...].reshape(RANK, ROWS)
    if until != 6:
        inverse = inverse_factor(dot_f32(factor, factor, ((1,), (1,))))
        small[0] = dot_f32(inverse, factor, ((1,), (0,)))
        small[1] = jnp.concatenate([inverse, jnp.zeros((RANK, 128 - RANK), F32)], axis=1)
    owners = [NZ * j // na for j in range(na)]
    owned = [z == zz for zz in owners]
    is_owner = functools.reduce(jnp.logical_or, owned)
    arrive(a_one.at[pl.ds(0, NY - 1)], 9)
    if until == 5 or until == 6:
        arrive(b_one.at[pl.ds(0, NZ - 1)], 8)
        return finish()
    a_sum[...] = functools.reduce(jnp.add, [a_one[k] for k in range(NY)])
    for j, zz in enumerate(owners):

        @pl.when(z != zz)
        def _(j=j, zz=zz):
            send(a_sum.at[j], a_two.at[z], 10, at(zz, y, c, x))

        @pl.when(z == zz)
        def _(j=j):
            a_two[z] = a_sum[j]

    arrive(b_one.at[pl.ds(0, NZ - 1)], 8)
    b_two[y] = functools.reduce(jnp.add, [b_one[k] for k in range(NZ)])
    for _, device in ys:
        send(b_two.at[y], b_two.at[y], 11, device)

    for j in range(na):

        @pl.when(owned[j])
        def _(j=j):
            drain(a_two.at[pl.ds(0, NZ - 1)], rsem.at[10])
            mine = ATOMS_B + na * y + j
            fin[c, mine] = functools.reduce(jnp.add, [a_two[k] for k in range(NZ)])
            for _, device in zs:
                send(fin.at[c, mine], fin.at[c, mine], 12, device)

    arrive(b_two.at[pl.ds(0, NY - 1)], 11)
    own_b = pl.ds(nb * z, nb)
    fin[c, own_b] = functools.reduce(jnp.add, [b_two[k] for k in range(NY)])
    for _, device in zs:
        send(fin.at[c, own_b], fin.at[c, own_b], 13, device)

    @pl.when(is_owner)
    def _():
        drain(a_sum.at[pl.ds(0, na - 1)], rsem.at[12])

    @pl.when(jnp.logical_not(is_owner))
    def _():
        drain(a_sum, rsem.at[12])

    own_a = pl.ds(ATOMS_B + na * y, na)
    for _, device in ys:
        send(fin.at[c, own_a], fin.at[c, own_a], 14, device)

    part_a, part_b = pl.ds(ATOMS_B, ATOMS_A), pl.ds(0, ATOMS_B)
    arrive(fin.at[c, pl.ds(0, ATOMS_A - na)], 14)
    send(fin.at[c, part_a], fin.at[c, part_a], 15, other)
    arrive(fin.at[c, pl.ds(0, ATOMS_B - nb)], 13)
    send(fin.at[c, part_b], fin.at[c, part_b], 16, other)
    arrive(fin.at[c, part_a], 15)
    arrive(fin.at[c, part_b], 16)

    @pl.when(is_owner)
    def _():
        drain(a_sum.at[pl.ds(0, na - 1)], ssem.at[10])
        drain(a_two.at[pl.ds(0, NZ - 1)], ssem.at[12])

    @pl.when(jnp.logical_not(is_owner))
    def _():
        drain(a_sum, ssem.at[10])

    finish()


def apply_kernel(ge, total, small, ortho_ref, q_ref, error_ref, qv, err, out_sem):
    ortho_t = small[0]
    ortho_ref[...] = ortho_t
    first = stack_left(small[1][:, :RANK])
    second = stack_left(jnp.swapaxes(ortho_t, 0, 1))
    outs = []
    for i, (t0, nt) in enumerate(CHUNKS):
        cols = pl.ds(t0 * 128, nt * 128)
        rows = [jnp.concatenate([total[r // 2, atom_of(t0 + t) + r % 2] for t in range(nt)], axis=1) for r in range(4)]
        q_next = jnp.dot(first, stack_right(jnp.concatenate(rows, axis=0)), preferred_element_type=F32) / REPLICAS
        qv[:, cols] = q_next
        outs.append(pltpu.make_async_copy(qv.at[:, cols], q_ref.at[:, cols], out_sem.at[2 * i]))
        outs[-1].start()
        approx = jnp.dot(second, stack_right(q_next), preferred_element_type=F32)
        merged = ge[pl.ds(0, ROWS), cols].astype(F32) + ge[pl.ds(ROWS, ROWS), cols].astype(F32)
        err[:, cols] = (merged - approx).astype(BF16)
        outs.append(pltpu.make_async_copy(err.at[:, cols], error_ref.at[0, :, cols], out_sem.at[2 * i + 1]))
        outs[-1].start()
    for copy in outs:
        copy.wait()


def stack_left(v):
    hi, mid, lo = split3(v)
    return jnp.concatenate([hi, hi, hi, mid, mid, lo], axis=1)


def stack_right(v):
    hi, mid, lo = split3(v)
    return jnp.concatenate([hi, mid, lo, hi, mid, hi], axis=0)


def atoms(*lead):
    return pltpu.VMEM((*lead, 8, 128), F32)


VMEM, HBM = pl.BlockSpec(memory_space=pltpu.VMEM), pl.BlockSpec(memory_space=pltpu.HBM)


def reduce_all(grads, error, q_t, until=None, collective_id=0, name="reduce_factors"):
    na, nb = ATOMS_A // NY, ATOMS_B // NZ
    return pl.pallas_call(
        functools.partial(reduce_kernel, until),
        out_shape=(
            jax.ShapeDtypeStruct((2 * ROWS, LOCAL), BF16),
            jax.ShapeDtypeStruct((2, ATOMS, 8, 128), F32),
            jax.ShapeDtypeStruct((2, RANK, 128), F32),
        ),
        in_specs=[HBM] * 3,
        out_specs=(VMEM, VMEM, VMEM),
        scratch_shapes=[
            pltpu.VMEM((RANK, LOCAL), F32),
            atoms(4), atoms(2 * NX, 2), atoms(NY, 2), atoms(NZ, 2), atoms(4),
            pltpu.VMEM((ROWS, LOCAL), F32), pltpu.VMEM((ROWS, LOCAL), F32), pltpu.VMEM((3 * ROWS, LOCAL), BF16), atoms(ATOMS),
            atoms(NY, na), atoms(NZ, nb), atoms(na), atoms(NZ), atoms(NY, nb),
            pltpu.SemaphoreType.DMA((3 * len(CHUNKS),)),
            pltpu.SemaphoreType.DMA((17,)),
            pltpu.SemaphoreType.DMA((17,)),
        ],
        compiler_params=pltpu.CompilerParams(collective_id=collective_id, has_side_effects=True, vmem_limit_bytes=32 * 2**20),
        name=name,
    )(*[pltpu.with_memory_space_constraint(v, pltpu.HBM) for v in (grads, error, q_t)])


def apply_all(ge, total, small):
    return pl.pallas_call(
        apply_kernel,
        out_shape=(
            jax.ShapeDtypeStruct((RANK, ROWS), F32),
            jax.ShapeDtypeStruct((RANK, LOCAL), F32),
            jax.ShapeDtypeStruct((1, ROWS, LOCAL), BF16),
        ),
        in_specs=[VMEM] * 3,
        out_specs=(VMEM, HBM, HBM),
        scratch_shapes=[
            pltpu.VMEM((RANK, LOCAL), F32),
            pltpu.VMEM((ROWS, LOCAL), BF16),
            pltpu.SemaphoreType.DMA((2 * len(CHUNKS),)),
        ],
        compiler_params=pltpu.CompilerParams(vmem_limit_bytes=20 * 2**20),
        name="apply_factors",
    )(ge, total, small)


def shards(grads, error, q_prev):
    ortho_t, q_t, error_next = apply_all(*reduce_all(grads, error, jnp.swapaxes(q_prev, 0, 1)))
    return jnp.swapaxes(ortho_t, 0, 1), jnp.swapaxes(q_t, 0, 1), error_next


def solution(mesh):
    in_specs = (P("rep", None, "tp"), P("rep", None, "tp"), P("tp", None))
    out_specs = (P(), P("tp", None), P("rep", None, "tp"))
    return jax.shard_map(shards, mesh=mesh, in_specs=in_specs, out_specs=out_specs, check_vma=False)
```

```python
import functools

import jax
import jax.numpy as jnp
from jax import lax
from jax.experimental import pallas as pl
from jax.experimental.pallas import tpu as pltpu
from jax.sharding import PartitionSpec as P

NZ, NY, NX = 12, 8, 4
ROWS, RANK = 128, 32
REPLICAS = 192
LOCAL = 5504
TILES = LOCAL // 128
ATOMS_A, ATOMS_B = 40, 48
TILES_B = 23
ATOMS = ATOMS_A + ATOMS_B
CHUNKS = ((0, 12), (12, 11), (23, 10), (33, 10))
PARTS = ((0, 23), (23, 20))
FIRST_STEPS = 20
MESH = pl.DeviceIdType.MESH
F32, BF16 = jnp.float32, jnp.bfloat16


def split3(v):
    hi = v.astype(BF16)
    rest = v - hi.astype(F32)
    mid = rest.astype(BF16)
    lo = (rest - mid.astype(F32)).astype(BF16)
    return hi, mid, lo


def atom_of(tile):
    return 2 * tile if tile < TILES_B else ATOMS_B + 2 * (tile - TILES_B)


def far_first(n):
    return sorted(range(1, n), key=lambda k: (-min(k, n - k), k))


def drain(ref, sem):
    pltpu.make_async_copy(ref, ref, sem).wait()


def dot_f32(a, b, dims):
    return lax.dot_general(a, b, (dims, ((), ())), precision=lax.Precision.HIGHEST, preferred_element_type=F32)


def start_elimination(gram):
    row = lax.broadcasted_iota(jnp.int32, (RANK, 128), 0)
    lane = lax.broadcasted_iota(jnp.int32, (RANK, 128), 1)
    work = jnp.concatenate([gram, jnp.zeros((RANK, 128 - RANK), F32)], axis=1)
    return work + (lane == row + RANK).astype(F32)


def eliminate(work, begin, end):
    row = lax.broadcasted_iota(jnp.int32, (RANK, 128), 0)
    lane = lax.broadcasted_iota(jnp.int32, (RANK, 128), 1)

    def step(k, work):
        column = jnp.sum(jnp.where(lane == k, work, 0.0), axis=1, keepdims=True)
        at_row = jnp.sum(jnp.where(row == k, work, 0.0), axis=0, keepdims=True)
        pivot = jnp.sum(jnp.where(row[:, :1] == k, column, 0.0), axis=0, keepdims=True)
        scale = lax.rsqrt(pivot)
        scale = scale * (1.5 - 0.5 * (pivot * scale) * scale)
        scaled = at_row * scale
        reduced = work - jnp.where(row[:, :1] > k, column * scale, 0.0) * scaled
        return jnp.where(row == k, scaled, reduced)

    return lax.fori_loop(begin, end, step, work)


def reduce_kernel(
    until, g_ref, e_ref, q_ref, ge, fin, ortho_ref, left_ref,
    qv, work, f_part, f_cx, f_y, f_z, f_full, m_own, m_other, pair, p_sum, a_one, b_one, a_sum, a_two, b_two,
    load_sem, ssem, rsem,
):
    rep, x = lax.axis_index("rep"), lax.axis_index("tp")
    c = lax.rem(rep, 2)
    y = lax.rem(rep // 2, NY)
    z = rep // (2 * NY)
    na, nb = ATOMS_A // NY, ATOMS_B // NZ

    def at(zz, yy, cc, xx):
        return {"rep": (zz * NY + yy) * 2 + cc, "tp": xx}

    other = at(z, y, 1 - c, x)
    xs = [(k, lax.rem(x + k, NX)) for k in far_first(NX)]
    cxs = [(lax.rem(c + flip, 2), at(z, y, lax.rem(c + flip, 2), xx)) for flip in (1, 0) for _, xx in xs]
    cxs.append((1 - c, other))
    ys = [(yy, at(z, yy, c, x)) for yy in [lax.rem(y + k, NY) for k in far_first(NY)]]
    zs = [(zz, at(zz, y, c, x)) for zz in [lax.rem(z + k, NZ) for k in far_first(NZ)]]
    sent = []

    def send(src, dst, sem, device):
        pltpu.make_async_remote_copy(
            src_ref=src, dst_ref=dst, send_sem=ssem.at[sem], recv_sem=rsem.at[sem], device_id=device, device_id_type=MESH
        ).start()

    def arrive(ref, sem):
        drain(ref, rsem.at[sem])
        sent.append((ref, sem))

    def finish():
        for ref, sem in sent:
            drain(ref, ssem.at[sem])

    barrier = pltpu.get_barrier_semaphore()
    partners = [d for _, d in zs] + [d for _, d in ys] + [d for _, d in cxs]
    for device in partners:
        pl.semaphore_signal(barrier, inc=1, device_id=device, device_id_type=MESH)

    loads = []
    for i, (t0, nt) in enumerate(PARTS):
        cols = pl.ds(t0 * 128, nt * 128)
        group = [
            pltpu.make_async_copy(q_ref.at[:, cols], qv.at[:, cols], load_sem.at[3 * i]),
            pltpu.make_async_copy(g_ref.at[0, :, cols], ge.at[pl.ds(0, ROWS), cols], load_sem.at[3 * i + 1]),
            pltpu.make_async_copy(e_ref.at[0, :, cols], ge.at[pl.ds(ROWS, ROWS), cols], load_sem.at[3 * i + 2]),
        ]
        for copy in group:
            copy.start()
        loads.append(group)

    both = jnp.zeros((3 * RANK, 2 * ROWS), F32)
    for (t0, nt), group in zip(PARTS, loads, strict=True):
        for copy in group:
            copy.wait()
        cols = pl.ds(t0 * 128, nt * 128)
        left = jnp.concatenate(split3(qv[:, cols]), axis=0)
        both += lax.dot_general(left, ge[:, cols], (((1,), (1,)), ((), ())), preferred_element_type=F32)
    both = both[:, :ROWS] + both[:, ROWS:]
    part = both[:RANK] + (both[RANK : 2 * RANK] + both[2 * RANK :])
    f_part[...] = part.reshape(4, 8, 128)
    pad = pl.ds(2 * TILES_B, ATOMS_B - 2 * TILES_B)
    p_sum[pad] = jnp.zeros((ATOMS_B - 2 * TILES_B, 8, 128), F32)
    pl.semaphore_wait(barrier, len(partners))
    if until == 0:
        return finish()

    own = 2 * x + c
    for cc, device in cxs:
        send(f_part.at[pl.ds(2 * cc, 2)], f_cx.at[own], 0, device)
    f_cx[own] = f_part[pl.ds(2 * c, 2)]
    for t0, nt in CHUNKS:
        cols = pl.ds(t0 * 128, nt * 128)
        m_own[:, cols] = ge[pl.ds(0, ROWS), cols].astype(F32) + ge[pl.ds(ROWS, ROWS), cols].astype(F32)
    arrive(f_cx.at[pl.ds(0, 2 * NX - 1)], 0)
    if until == 1:
        return finish()
    f_y[y] = functools.reduce(jnp.add, [f_cx[k] for k in range(2 * NX)])
    for _, device in ys:
        send(f_y.at[y], f_y.at[y], 1, device)
    for i, (t0, nt) in enumerate(CHUNKS):
        cols = pl.ds(t0 * 128, nt * 128)
        send(m_own.at[:, cols], m_other.at[:, cols], 4 + i, other)
    arrive(f_y.at[pl.ds(0, NY - 1)], 1)
    if until == 2:
        return finish()
    f_z[z] = functools.reduce(jnp.add, [f_y[k] for k in range(NY)])
    for _, device in zs:
        send(f_z.at[z], f_z.at[z], 2, device)
    for i, (t0, nt) in enumerate(CHUNKS):
        cols = pl.ds(t0 * 128, nt * 128)
        arrive(m_other.at[:, cols], 4 + i)
        for k, piece in enumerate(split3(m_own[:, cols] + m_other[:, cols])):
            pair[pl.ds(ROWS * k, ROWS), cols] = piece
    arrive(f_z.at[pl.ds(0, NZ - 1)], 2)
    if until == 3:
        return finish()
    half = pl.ds(2 * c, 2)
    f_full[half] = functools.reduce(jnp.add, [f_z[k] for k in range(NZ)])
    send(f_full.at[half], f_full.at[half], 3, other)
    if until == 4:
        arrive(f_full.at[pl.ds(0, 2)], 3)
        return finish()

    left = jnp.concatenate(split3(f_full[half].reshape(RANK // 2, ROWS)), axis=0)
    left = jnp.concatenate([left, left, left], axis=1)

    def project(i):
        t0, nt = PARTS[i]
        three = jnp.dot(left, pair[:, pl.ds(t0 * 128, nt * 128)], preferred_element_type=F32)
        term = three[:16] + (three[16:32] + three[32:])
        for t in range(nt):
            for r in range(2):
                p_sum[atom_of(t0 + t) + r] = term[8 * r : 8 * r + 8, 128 * t : 128 * t + 128]

    project(0)
    for zz, device in zs:
        send(p_sum.at[pl.ds(nb * zz, nb)], b_one.at[z], 8, device)
    b_one[z] = p_sum[pl.ds(nb * z, nb)]
    project(1)
    for yy, device in ys:
        send(p_sum.at[pl.ds(ATOMS_B + na * yy, na)], a_one.at[y], 9, device)
    a_one[y] = p_sum[pl.ds(ATOMS_B + na * y, na)]

    arrive(f_full.at[pl.ds(0, 2)], 3)
    factor = f_full[...].reshape(RANK, ROWS)
    work[...] = eliminate(start_elimination(dot_f32(factor, factor, ((1,), (1,)))), 0, FIRST_STEPS)
    owners = [NZ * j // na for j in range(na)]
    owned = [z == zz for zz in owners]
    is_owner = functools.reduce(jnp.logical_or, owned)
    arrive(a_one.at[pl.ds(0, NY - 1)], 9)
    if until == 5 or until == 6:
        arrive(b_one.at[pl.ds(0, NZ - 1)], 8)
        return finish()
    a_sum[...] = functools.reduce(jnp.add, [a_one[k] for k in range(NY)])
    for j, zz in enumerate(owners):

        @pl.when(z != zz)
        def _(j=j, zz=zz):
            send(a_sum.at[j], a_two.at[z], 10, at(zz, y, c, x))

        @pl.when(z == zz)
        def _(j=j):
            a_two[z] = a_sum[j]

    arrive(b_one.at[pl.ds(0, NZ - 1)], 8)
    b_two[y] = functools.reduce(jnp.add, [b_one[k] for k in range(NZ)])
    for _, device in ys:
        send(b_two.at[y], b_two.at[y], 11, device)

    for j in range(na):

        @pl.when(owned[j])
        def _(j=j):
            drain(a_two.at[pl.ds(0, NZ - 1)], rsem.at[10])
            mine = ATOMS_B + na * y + j
            fin[c, mine] = functools.reduce(jnp.add, [a_two[k] for k in range(NZ)])
            for _, device in zs:
                send(fin.at[c, mine], fin.at[c, mine], 12, device)

    arrive(b_two.at[pl.ds(0, NY - 1)], 11)
    own_b = pl.ds(nb * z, nb)
    fin[c, own_b] = functools.reduce(jnp.add, [b_two[k] for k in range(NY)])
    for _, device in zs:
        send(fin.at[c, own_b], fin.at[c, own_b], 13, device)

    @pl.when(is_owner)
    def _():
        drain(a_sum.at[pl.ds(0, na - 1)], rsem.at[12])

    @pl.when(jnp.logical_not(is_owner))
    def _():
        drain(a_sum, rsem.at[12])

    own_a = pl.ds(ATOMS_B + na * y, na)
    for _, device in ys:
        send(fin.at[c, own_a], fin.at[c, own_a], 14, device)

    inverse = eliminate(work[...], FIRST_STEPS, RANK)[:, RANK : 2 * RANK]
    ortho_t = dot_f32(inverse, factor, ((1,), (0,)))
    ortho_ref[...] = ortho_t
    weights = jnp.concatenate([inverse, dot_f32(jnp.swapaxes(ortho_t, 0, 1), inverse, ((1,), (0,)))], axis=0)
    hi, mid, lo = split3(weights * (1.0 / REPLICAS))
    left_ref[...] = jnp.concatenate([hi, hi, hi, mid, mid, lo], axis=1)

    part_a, part_b = pl.ds(ATOMS_B, ATOMS_A), pl.ds(0, ATOMS_B)
    arrive(fin.at[c, pl.ds(0, ATOMS_A - na)], 14)
    send(fin.at[c, part_a], fin.at[c, part_a], 15, other)
    arrive(fin.at[c, pl.ds(0, ATOMS_B - nb)], 13)
    send(fin.at[c, part_b], fin.at[c, part_b], 16, other)
    arrive(fin.at[c, part_a], 15)
    arrive(fin.at[c, part_b], 16)

    @pl.when(is_owner)
    def _():
        drain(a_sum.at[pl.ds(0, na - 1)], ssem.at[10])
        drain(a_two.at[pl.ds(0, NZ - 1)], ssem.at[12])

    @pl.when(jnp.logical_not(is_owner))
    def _():
        drain(a_sum, ssem.at[10])

    finish()


def apply_kernel(ge, total, ortho, left, ortho_ref, q_ref, error_ref, qv, err, out_sem):
    ortho_ref[...] = ortho[...]
    outs = []
    for i, (t0, nt) in enumerate(CHUNKS):
        cols = pl.ds(t0 * 128, nt * 128)
        rows = [jnp.concatenate([total[r // 2, atom_of(t0 + t) + r % 2] for t in range(nt)], axis=1) for r in range(4)]
        both = jnp.dot(left[...], stack_right(jnp.concatenate(rows, axis=0)), preferred_element_type=F32)
        qv[:, cols] = both[:RANK]
        merged = ge[pl.ds(0, ROWS), cols].astype(F32) + ge[pl.ds(ROWS, ROWS), cols].astype(F32)
        err[:, cols] = (merged - both[RANK:]).astype(BF16)
        group = [
            pltpu.make_async_copy(qv.at[:, cols], q_ref.at[:, cols], out_sem.at[2 * i]),
            pltpu.make_async_copy(err.at[:, cols], error_ref.at[0, :, cols], out_sem.at[2 * i + 1]),
        ]
        for copy in group:
            copy.start()
        outs += group
    for copy in outs:
        copy.wait()


def stack_right(v):
    hi, mid, lo = split3(v)
    return jnp.concatenate([hi, mid, lo, hi, mid, hi], axis=0)


def atoms(*lead):
    return pltpu.VMEM((*lead, 8, 128), F32)


VMEM, HBM = pl.BlockSpec(memory_space=pltpu.VMEM), pl.BlockSpec(memory_space=pltpu.HBM)


def reduce_all(grads, error, q_t, until=None, collective_id=0, name="reduce_factors"):
    na, nb = ATOMS_A // NY, ATOMS_B // NZ
    return pl.pallas_call(
        functools.partial(reduce_kernel, until),
        out_shape=(
            jax.ShapeDtypeStruct((2 * ROWS, LOCAL), BF16),
            jax.ShapeDtypeStruct((2, ATOMS, 8, 128), F32),
            jax.ShapeDtypeStruct((RANK, ROWS), F32),
            jax.ShapeDtypeStruct((RANK + ROWS, 6 * RANK), BF16),
        ),
        in_specs=[HBM] * 3,
        out_specs=(VMEM,) * 4,
        scratch_shapes=[
            pltpu.VMEM((RANK, LOCAL), F32),
            pltpu.VMEM((RANK, 128), F32),
            atoms(4), atoms(2 * NX, 2), atoms(NY, 2), atoms(NZ, 2), atoms(4),
            pltpu.VMEM((ROWS, LOCAL), F32), pltpu.VMEM((ROWS, LOCAL), F32), pltpu.VMEM((3 * ROWS, LOCAL), BF16), atoms(ATOMS),
            atoms(NY, na), atoms(NZ, nb), atoms(na), atoms(NZ), atoms(NY, nb),
            pltpu.SemaphoreType.DMA((3 * len(PARTS),)),
            pltpu.SemaphoreType.DMA((17,)),
            pltpu.SemaphoreType.DMA((17,)),
        ],
        compiler_params=pltpu.CompilerParams(collective_id=collective_id, has_side_effects=True, vmem_limit_bytes=32 * 2**20),
        name=name,
    )(*[pltpu.with_memory_space_constraint(v, pltpu.HBM) for v in (grads, error, q_t)])


def apply_all(ge, total, ortho_t, left):
    return pl.pallas_call(
        apply_kernel,
        out_shape=(
            jax.ShapeDtypeStruct((RANK, ROWS), F32),
            jax.ShapeDtypeStruct((RANK, LOCAL), F32),
            jax.ShapeDtypeStruct((1, ROWS, LOCAL), BF16),
        ),
        in_specs=[VMEM] * 4,
        out_specs=(VMEM, HBM, HBM),
        scratch_shapes=[
            pltpu.VMEM((RANK, LOCAL), F32),
            pltpu.VMEM((ROWS, LOCAL), BF16),
            pltpu.SemaphoreType.DMA((2 * len(CHUNKS),)),
        ],
        compiler_params=pltpu.CompilerParams(vmem_limit_bytes=20 * 2**20),
        name="apply_factors",
    )(ge, total, ortho_t, left)


def shards(grads, error, q_prev):
    ortho_t, q_t, error_next = apply_all(*reduce_all(grads, error, jnp.swapaxes(q_prev, 0, 1)))
    return jnp.swapaxes(ortho_t, 0, 1), jnp.swapaxes(q_t, 0, 1), error_next


def solution(mesh):
    in_specs = (P("rep", None, "tp"), P("rep", None, "tp"), P("tp", None))
    out_specs = (P(), P("tp", None), P("rep", None, "tp"))
    return jax.shard_map(shards, mesh=mesh, in_specs=in_specs, out_specs=out_specs, check_vma=False)
```

```python
import functools

import jax
import jax.numpy as jnp
from jax import lax
from jax.experimental import pallas as pl
from jax.experimental.pallas import tpu as pltpu
from jax.sharding import PartitionSpec as P

NZ, NY, NX = 12, 8, 4
ROWS, RANK = 128, 32
REPLICAS = 192
LOCAL = 5504
TILES = LOCAL // 128
ATOMS_A, ATOMS_B = 40, 48
TILES_B = 23
ATOMS = ATOMS_A + ATOMS_B
CHUNKS = ((0, 12), (12, 11), (23, 10), (33, 10))
PARTS = ((0, 23), (23, 20))
FIRST_STEPS = 20
MESH = pl.DeviceIdType.MESH
F32, BF16 = jnp.float32, jnp.bfloat16


def split3(v):
    hi = v.astype(BF16)
    rest = v - hi.astype(F32)
    mid = rest.astype(BF16)
    lo = (rest - mid.astype(F32)).astype(BF16)
    return hi, mid, lo


def atom_of(tile):
    return 2 * tile if tile < TILES_B else ATOMS_B + 2 * (tile - TILES_B)


def far_first(n):
    return sorted(range(1, n), key=lambda k: (-min(k, n - k), k))


def drain(ref, sem):
    pltpu.make_async_copy(ref, ref, sem).wait()


def dot_f32(a, b, dims):
    return lax.dot_general(a, b, (dims, ((), ())), precision=lax.Precision.HIGHEST, preferred_element_type=F32)


def start_elimination(gram):
    row = lax.broadcasted_iota(jnp.int32, (RANK, 128), 0)
    lane = lax.broadcasted_iota(jnp.int32, (RANK, 128), 1)
    work = jnp.concatenate([gram, jnp.zeros((RANK, 128 - RANK), F32)], axis=1)
    return work + (lane == row + RANK).astype(F32)


def eliminate(work, begin, end):
    row = lax.broadcasted_iota(jnp.int32, (RANK, 128), 0)
    lane = lax.broadcasted_iota(jnp.int32, (RANK, 128), 1)

    def step(k, work):
        column = jnp.sum(jnp.where(lane == k, work, 0.0), axis=1, keepdims=True)
        at_row = jnp.sum(jnp.where(row == k, work, 0.0), axis=0, keepdims=True)
        pivot = jnp.sum(jnp.where(row[:, :1] == k, column, 0.0), axis=0, keepdims=True)
        scale = lax.rsqrt(pivot)
        scale = scale * (1.5 - 0.5 * (pivot * scale) * scale)
        scaled = at_row * scale
        reduced = work - jnp.where(row[:, :1] > k, column * scale, 0.0) * scaled
        return jnp.where(row == k, scaled, reduced)

    return lax.fori_loop(begin, end, step, work)


def reduce_kernel(
    until, g_ref, e_ref, q_ref, ge, fin, ortho_ref, left_ref,
    qv, work, f_part, f_cx, f_y, f_z, f_full, m_own, m_other, pair, p_sum, a_one, b_one, a_sum, a_two, b_two,
    load_sem, ssem, rsem,
):
    rep, x = lax.axis_index("rep"), lax.axis_index("tp")
    c = lax.rem(rep, 2)
    y = lax.rem(rep // 2, NY)
    z = rep // (2 * NY)
    na, nb = ATOMS_A // NY, ATOMS_B // NZ

    def at(zz, yy, cc, xx):
        return {"rep": (zz * NY + yy) * 2 + cc, "tp": xx}

    other = at(z, y, 1 - c, x)
    xs = [(k, lax.rem(x + k, NX)) for k in far_first(NX)]
    cxs = [(lax.rem(c + flip, 2), at(z, y, lax.rem(c + flip, 2), xx)) for flip in (1, 0) for _, xx in xs]
    cxs.append((1 - c, other))
    ys = [(yy, at(z, yy, c, x)) for yy in [lax.rem(y + k, NY) for k in far_first(NY)]]
    zs = [(zz, at(zz, y, c, x)) for zz in [lax.rem(z + k, NZ) for k in far_first(NZ)]]
    sent = []

    def send(src, dst, sem, device):
        pltpu.make_async_remote_copy(
            src_ref=src, dst_ref=dst, send_sem=ssem.at[sem], recv_sem=rsem.at[sem], device_id=device, device_id_type=MESH
        ).start()

    def arrive(ref, sem):
        drain(ref, rsem.at[sem])
        sent.append((ref, sem))

    def finish():
        for ref, sem in sent:
            drain(ref, ssem.at[sem])

    barrier = pltpu.get_barrier_semaphore()
    partners = [d for _, d in zs] + [d for _, d in ys] + [d for _, d in cxs]
    for device in partners:
        pl.semaphore_signal(barrier, inc=1, device_id=device, device_id_type=MESH)

    loads = []
    for i, (t0, nt) in enumerate(PARTS):
        cols = pl.ds(t0 * 128, nt * 128)
        group = [
            pltpu.make_async_copy(q_ref.at[:, cols], qv.at[:, cols], load_sem.at[3 * i]),
            pltpu.make_async_copy(g_ref.at[0, :, cols], ge.at[pl.ds(0, ROWS), cols], load_sem.at[3 * i + 1]),
            pltpu.make_async_copy(e_ref.at[0, :, cols], ge.at[pl.ds(ROWS, ROWS), cols], load_sem.at[3 * i + 2]),
        ]
        for copy in group:
            copy.start()
        loads.append(group)

    both = jnp.zeros((3 * RANK, 2 * ROWS), F32)
    for (t0, nt), group in zip(PARTS, loads, strict=True):
        for copy in group:
            copy.wait()
        cols = pl.ds(t0 * 128, nt * 128)
        left = jnp.concatenate(split3(qv[:, cols]), axis=0)
        both += lax.dot_general(left, ge[:, cols], (((1,), (1,)), ((), ())), preferred_element_type=F32)
    both = both[:, :ROWS] + both[:, ROWS:]
    part = both[:RANK] + (both[RANK : 2 * RANK] + both[2 * RANK :])
    f_part[...] = part.reshape(4, 8, 128)
    pad = pl.ds(2 * TILES_B, ATOMS_B - 2 * TILES_B)
    p_sum[pad] = jnp.zeros((ATOMS_B - 2 * TILES_B, 8, 128), F32)
    pl.semaphore_wait(barrier, len(partners))
    if until == 0:
        return finish()

    own = 2 * x + c
    for cc, device in cxs:
        send(f_part.at[pl.ds(2 * cc, 2)], f_cx.at[own], 0, device)
    f_cx[own] = f_part[pl.ds(2 * c, 2)]
    for t0, nt in CHUNKS:
        cols = pl.ds(t0 * 128, nt * 128)
        m_own[:, cols] = ge[pl.ds(0, ROWS), cols].astype(F32) + ge[pl.ds(ROWS, ROWS), cols].astype(F32)
    arrive(f_cx.at[pl.ds(0, 2 * NX - 1)], 0)
    if until == 1:
        return finish()
    f_y[y] = functools.reduce(jnp.add, [f_cx[k] for k in range(2 * NX)])
    for _, device in ys:
        send(f_y.at[y], f_y.at[y], 1, device)
    for i, (t0, nt) in enumerate(CHUNKS):
        cols = pl.ds(t0 * 128, nt * 128)
        send(m_own.at[:, cols], m_other.at[:, cols], 4 + i, other)
    arrive(f_y.at[pl.ds(0, NY - 1)], 1)
    if until == 2:
        return finish()
    f_z[z] = functools.reduce(jnp.add, [f_y[k] for k in range(NY)])
    for _, device in zs:
        send(f_z.at[z], f_z.at[z], 2, device)
    for i, (t0, nt) in enumerate(CHUNKS):
        cols = pl.ds(t0 * 128, nt * 128)
        arrive(m_other.at[:, cols], 4 + i)
        for k, piece in enumerate(split3(m_own[:, cols] + m_other[:, cols])):
            pair[pl.ds(ROWS * k, ROWS), cols] = piece
    arrive(f_z.at[pl.ds(0, NZ - 1)], 2)
    if until == 3:
        return finish()
    half = pl.ds(2 * c, 2)
    f_full[half] = functools.reduce(jnp.add, [f_z[k] for k in range(NZ)])
    send(f_full.at[half], f_full.at[half], 3, other)
    if until == 4:
        arrive(f_full.at[pl.ds(0, 2)], 3)
        return finish()

    left = jnp.concatenate(split3(f_full[half].reshape(RANK // 2, ROWS)), axis=0)
    left = jnp.concatenate([left, left, left], axis=1)

    def project(i):
        t0, nt = PARTS[i]
        three = jnp.dot(left, pair[:, pl.ds(t0 * 128, nt * 128)], preferred_element_type=F32)
        term = three[:16] + (three[16:32] + three[32:])
        for t in range(nt):
            for r in range(2):
                p_sum[atom_of(t0 + t) + r] = term[8 * r : 8 * r + 8, 128 * t : 128 * t + 128]

    project(1)
    for yy, device in ys:
        send(p_sum.at[pl.ds(ATOMS_B + na * yy, na)], a_one.at[y], 9, device)
    a_one[y] = p_sum[pl.ds(ATOMS_B + na * y, na)]
    project(0)
    for zz, device in zs:
        send(p_sum.at[pl.ds(nb * zz, nb)], b_one.at[z], 8, device)
    b_one[z] = p_sum[pl.ds(nb * z, nb)]

    arrive(f_full.at[pl.ds(0, 2)], 3)
    factor = f_full[...].reshape(RANK, ROWS)
    work[...] = eliminate(start_elimination(dot_f32(factor, factor, ((1,), (1,)))), 0, FIRST_STEPS)
    owners = [NZ * j // na for j in range(na)]
    owned = [z == zz for zz in owners]
    is_owner = functools.reduce(jnp.logical_or, owned)
    arrive(a_one.at[pl.ds(0, NY - 1)], 9)
    if until == 5 or until == 6:
        arrive(b_one.at[pl.ds(0, NZ - 1)], 8)
        return finish()
    a_sum[...] = functools.reduce(jnp.add, [a_one[k] for k in range(NY)])
    for j, zz in enumerate(owners):

        @pl.when(z != zz)
        def _(j=j, zz=zz):
            send(a_sum.at[j], a_two.at[z], 10, at(zz, y, c, x))

        @pl.when(z == zz)
        def _(j=j):
            a_two[z] = a_sum[j]

    arrive(b_one.at[pl.ds(0, NZ - 1)], 8)
    b_two[y] = functools.reduce(jnp.add, [b_one[k] for k in range(NZ)])
    for _, device in ys:
        send(b_two.at[y], b_two.at[y], 11, device)

    for j in range(na):

        @pl.when(owned[j])
        def _(j=j):
            drain(a_two.at[pl.ds(0, NZ - 1)], rsem.at[10])
            mine = ATOMS_B + na * y + j
            fin[c, mine] = functools.reduce(jnp.add, [a_two[k] for k in range(NZ)])
            for _, device in zs:
                send(fin.at[c, mine], fin.at[c, mine], 12, device)

    arrive(b_two.at[pl.ds(0, NY - 1)], 11)
    own_b = pl.ds(nb * z, nb)
    fin[c, own_b] = functools.reduce(jnp.add, [b_two[k] for k in range(NY)])
    for _, device in zs:
        send(fin.at[c, own_b], fin.at[c, own_b], 13, device)

    @pl.when(is_owner)
    def _():
        drain(a_sum.at[pl.ds(0, na - 1)], rsem.at[12])

    @pl.when(jnp.logical_not(is_owner))
    def _():
        drain(a_sum, rsem.at[12])

    own_a = pl.ds(ATOMS_B + na * y, na)
    for _, device in ys:
        send(fin.at[c, own_a], fin.at[c, own_a], 14, device)

    inverse = eliminate(work[...], FIRST_STEPS, RANK)[:, RANK : 2 * RANK]
    ortho_t = dot_f32(inverse, factor, ((1,), (0,)))
    ortho_ref[...] = ortho_t
    weights = jnp.concatenate([inverse, dot_f32(jnp.swapaxes(ortho_t, 0, 1), inverse, ((1,), (0,)))], axis=0)
    hi, mid, lo = split3(weights * (1.0 / REPLICAS))
    left_ref[...] = jnp.concatenate([hi, hi, hi, mid, mid, lo], axis=1)

    part_a, part_b = pl.ds(ATOMS_B, ATOMS_A), pl.ds(0, ATOMS_B)
    arrive(fin.at[c, pl.ds(0, ATOMS_A - na)], 14)
    send(fin.at[c, part_a], fin.at[c, part_a], 15, other)
    arrive(fin.at[c, pl.ds(0, ATOMS_B - nb)], 13)
    send(fin.at[c, part_b], fin.at[c, part_b], 16, other)
    arrive(fin.at[c, part_a], 15)
    arrive(fin.at[c, part_b], 16)

    @pl.when(is_owner)
    def _():
        drain(a_sum.at[pl.ds(0, na - 1)], ssem.at[10])
        drain(a_two.at[pl.ds(0, NZ - 1)], ssem.at[12])

    @pl.when(jnp.logical_not(is_owner))
    def _():
        drain(a_sum, ssem.at[10])

    finish()


def apply_kernel(ge, total, ortho, left, ortho_ref, q_ref, error_ref, qv, err, out_sem):
    ortho_ref[...] = ortho[...]
    outs = []
    for i, (t0, nt) in enumerate(CHUNKS):
        cols = pl.ds(t0 * 128, nt * 128)
        rows = [jnp.concatenate([total[r // 2, atom_of(t0 + t) + r % 2] for t in range(nt)], axis=1) for r in range(4)]
        both = jnp.dot(left[...], stack_right(jnp.concatenate(rows, axis=0)), preferred_element_type=F32)
        qv[:, cols] = both[:RANK]
        merged = ge[pl.ds(0, ROWS), cols].astype(F32) + ge[pl.ds(ROWS, ROWS), cols].astype(F32)
        err[:, cols] = (merged - both[RANK:]).astype(BF16)
        group = [
            pltpu.make_async_copy(qv.at[:, cols], q_ref.at[:, cols], out_sem.at[2 * i]),
            pltpu.make_async_copy(err.at[:, cols], error_ref.at[0, :, cols], out_sem.at[2 * i + 1]),
        ]
        for copy in group:
            copy.start()
        outs += group
    for copy in outs:
        copy.wait()


def stack_right(v):
    hi, mid, lo = split3(v)
    return jnp.concatenate([hi, mid, lo, hi, mid, hi], axis=0)


def atoms(*lead):
    return pltpu.VMEM((*lead, 8, 128), F32)


VMEM, HBM = pl.BlockSpec(memory_space=pltpu.VMEM), pl.BlockSpec(memory_space=pltpu.HBM)


def reduce_all(grads, error, q_t, until=None, collective_id=0, name="reduce_factors"):
    na, nb = ATOMS_A // NY, ATOMS_B // NZ
    return pl.pallas_call(
        functools.partial(reduce_kernel, until),
        out_shape=(
            jax.ShapeDtypeStruct((2 * ROWS, LOCAL), BF16),
            jax.ShapeDtypeStruct((2, ATOMS, 8, 128), F32),
            jax.ShapeDtypeStruct((RANK, ROWS), F32),
            jax.ShapeDtypeStruct((RANK + ROWS, 6 * RANK), BF16),
        ),
        in_specs=[HBM] * 3,
        out_specs=(VMEM,) * 4,
        scratch_shapes=[
            pltpu.VMEM((RANK, LOCAL), F32),
            pltpu.VMEM((RANK, 128), F32),
            atoms(4), atoms(2 * NX, 2), atoms(NY, 2), atoms(NZ, 2), atoms(4),
            pltpu.VMEM((ROWS, LOCAL), F32), pltpu.VMEM((ROWS, LOCAL), F32), pltpu.VMEM((3 * ROWS, LOCAL), BF16), atoms(ATOMS),
            atoms(NY, na), atoms(NZ, nb), atoms(na), atoms(NZ), atoms(NY, nb),
            pltpu.SemaphoreType.DMA((3 * len(PARTS),)),
            pltpu.SemaphoreType.DMA((17,)),
            pltpu.SemaphoreType.DMA((17,)),
        ],
        compiler_params=pltpu.CompilerParams(collective_id=collective_id, has_side_effects=True, vmem_limit_bytes=32 * 2**20),
        name=name,
    )(*[pltpu.with_memory_space_constraint(v, pltpu.HBM) for v in (grads, error, q_t)])


def apply_all(ge, total, ortho_t, left):
    return pl.pallas_call(
        apply_kernel,
        out_shape=(
            jax.ShapeDtypeStruct((RANK, ROWS), F32),
            jax.ShapeDtypeStruct((RANK, LOCAL), F32),
            jax.ShapeDtypeStruct((1, ROWS, LOCAL), BF16),
        ),
        in_specs=[VMEM] * 4,
        out_specs=(VMEM, HBM, HBM),
        scratch_shapes=[
            pltpu.VMEM((RANK, LOCAL), F32),
            pltpu.VMEM((ROWS, LOCAL), BF16),
            pltpu.SemaphoreType.DMA((2 * len(CHUNKS),)),
        ],
        compiler_params=pltpu.CompilerParams(vmem_limit_bytes=20 * 2**20),
        name="apply_factors",
    )(ge, total, ortho_t, left)


def shards(grads, error, q_prev):
    ortho_t, q_t, error_next = apply_all(*reduce_all(grads, error, jnp.swapaxes(q_prev, 0, 1)))
    return jnp.swapaxes(ortho_t, 0, 1), jnp.swapaxes(q_t, 0, 1), error_next


def solution(mesh):
    in_specs = (P("rep", None, "tp"), P("rep", None, "tp"), P("tp", None))
    out_specs = (P(), P("tp", None), P("rep", None, "tp"))
    return jax.shard_map(shards, mesh=mesh, in_specs=in_specs, out_specs=out_specs, check_vma=False)
```

```python
import functools

import jax
import jax.numpy as jnp
from jax import lax
from jax.experimental import pallas as pl
from jax.experimental.pallas import tpu as pltpu
from jax.sharding import PartitionSpec as P

NZ, NY, NX = 12, 8, 4
ROWS, RANK = 128, 32
REPLICAS = 192
LOCAL = 5504
TILES = LOCAL // 128
ATOMS_A, ATOMS_B = 40, 48
TILES_B = 23
ATOMS = ATOMS_A + ATOMS_B
CHUNKS = ((0, 12), (12, 11), (23, 10), (33, 10))
PARTS = ((0, 23), (23, 20))
FIRST_STEPS = 20
MESH = pl.DeviceIdType.MESH
F32, BF16 = jnp.float32, jnp.bfloat16


def split3(v):
    hi = v.astype(BF16)
    rest = v - hi.astype(F32)
    mid = rest.astype(BF16)
    lo = (rest - mid.astype(F32)).astype(BF16)
    return hi, mid, lo


def atom_of(tile):
    return 2 * tile if tile < TILES_B else ATOMS_B + 2 * (tile - TILES_B)


def far_first(n):
    return sorted(range(1, n), key=lambda k: (-min(k, n - k), k))


def drain(ref, sem):
    pltpu.make_async_copy(ref, ref, sem).wait()


def dot_f32(a, b, dims):
    return lax.dot_general(a, b, (dims, ((), ())), precision=lax.Precision.HIGHEST, preferred_element_type=F32)


def start_elimination(gram):
    row = lax.broadcasted_iota(jnp.int32, (RANK, 128), 0)
    lane = lax.broadcasted_iota(jnp.int32, (RANK, 128), 1)
    work = jnp.concatenate([gram, jnp.zeros((RANK, 128 - RANK), F32)], axis=1)
    return work + (lane == row + RANK).astype(F32)


def eliminate(work, begin, end):
    row = lax.broadcasted_iota(jnp.int32, (RANK, 128), 0)
    lane = lax.broadcasted_iota(jnp.int32, (RANK, 128), 1)

    def step(k, work):
        column = jnp.sum(jnp.where(lane == k, work, 0.0), axis=1, keepdims=True)
        at_row = jnp.sum(jnp.where(row == k, work, 0.0), axis=0, keepdims=True)
        pivot = jnp.sum(jnp.where(row[:, :1] == k, column, 0.0), axis=0, keepdims=True)
        scale = lax.rsqrt(pivot)
        scale = scale * (1.5 - 0.5 * (pivot * scale) * scale)
        scaled = at_row * scale
        reduced = work - jnp.where(row[:, :1] > k, column * scale, 0.0) * scaled
        return jnp.where(row == k, scaled, reduced)

    return lax.fori_loop(begin, end, step, work)


def reduce_kernel(
    g_ref, e_ref, q_ref, ge, fin, ortho_ref, left_ref,
    qv, work, f_part, f_cx, f_y, f_z, f_full, m_own, m_other, pair, p_sum, a_one, b_one, a_two, b_two,
    load_sem, ssem, rsem,
):
    rep, x = lax.axis_index("rep"), lax.axis_index("tp")
    c = lax.rem(rep, 2)
    y = lax.rem(rep // 2, NY)
    z = rep // (2 * NY)
    na, nb = ATOMS_A // NY, ATOMS_B // NZ

    def at(zz, yy, cc, xx):
        return {"rep": (zz * NY + yy) * 2 + cc, "tp": xx}

    other = at(z, y, 1 - c, x)
    xs = [(k, lax.rem(x + k, NX)) for k in far_first(NX)]
    cxs = [(lax.rem(c + flip, 2), at(z, y, lax.rem(c + flip, 2), xx)) for flip in (1, 0) for _, xx in xs]
    cxs.append((1 - c, other))
    ys = [(yy, at(z, yy, c, x)) for yy in [lax.rem(y + k, NY) for k in far_first(NY)]]
    zs = [(zz, at(zz, y, c, x)) for zz in [lax.rem(z + k, NZ) for k in far_first(NZ)]]
    sent = []

    def send(src, dst, sem, device):
        pltpu.make_async_remote_copy(
            src_ref=src, dst_ref=dst, send_sem=ssem.at[sem], recv_sem=rsem.at[sem], device_id=device, device_id_type=MESH
        ).start()

    def arrive(ref, sem):
        drain(ref, rsem.at[sem])
        sent.append((ref, sem))

    def finish():
        while sent:
            ref, sem = sent.pop(0)
            drain(ref, ssem.at[sem])

    barrier = pltpu.get_barrier_semaphore()
    partners = [d for _, d in zs] + [d for _, d in ys] + [d for _, d in cxs]
    for device in partners:
        pl.semaphore_signal(barrier, inc=1, device_id=device, device_id_type=MESH)

    loads = []
    for i, (t0, nt) in enumerate(PARTS):
        cols = pl.ds(t0 * 128, nt * 128)
        group = [
            pltpu.make_async_copy(q_ref.at[:, cols], qv.at[:, cols], load_sem.at[3 * i]),
            pltpu.make_async_copy(g_ref.at[0, :, cols], ge.at[pl.ds(0, ROWS), cols], load_sem.at[3 * i + 1]),
            pltpu.make_async_copy(e_ref.at[0, :, cols], ge.at[pl.ds(ROWS, ROWS), cols], load_sem.at[3 * i + 2]),
        ]
        for copy in group:
            copy.start()
        loads.append(group)

    both = jnp.zeros((3 * RANK, 2 * ROWS), F32)
    for (t0, nt), group in zip(PARTS, loads, strict=True):
        for copy in group:
            copy.wait()
        cols = pl.ds(t0 * 128, nt * 128)
        left = jnp.concatenate(split3(qv[:, cols]), axis=0)
        both += lax.dot_general(left, ge[:, cols], (((1,), (1,)), ((), ())), preferred_element_type=F32)
    both = both[:, :ROWS] + both[:, ROWS:]
    part = both[:RANK] + (both[RANK : 2 * RANK] + both[2 * RANK :])
    f_part[...] = part.reshape(4, 8, 128)
    pad = pl.ds(2 * TILES_B, ATOMS_B - 2 * TILES_B)
    p_sum[pad] = jnp.zeros((ATOMS_B - 2 * TILES_B, 8, 128), F32)
    pl.semaphore_wait(barrier, len(partners))

    own = 2 * x + c
    for cc, device in cxs:
        send(f_part.at[pl.ds(2 * cc, 2)], f_cx.at[own], 0, device)
    f_cx[own] = f_part[pl.ds(2 * c, 2)]
    for t0, nt in CHUNKS:
        cols = pl.ds(t0 * 128, nt * 128)
        m_own[:, cols] = ge[pl.ds(0, ROWS), cols].astype(F32) + ge[pl.ds(ROWS, ROWS), cols].astype(F32)
    arrive(f_cx.at[pl.ds(0, 2 * NX - 1)], 0)
    f_y[y] = functools.reduce(jnp.add, [f_cx[k] for k in range(2 * NX)])
    for _, device in ys:
        send(f_y.at[y], f_y.at[y], 1, device)
    for i, (t0, nt) in enumerate(CHUNKS):
        cols = pl.ds(t0 * 128, nt * 128)
        send(m_own.at[:, cols], m_other.at[:, cols], 4 + i, other)
    arrive(f_y.at[pl.ds(0, NY - 1)], 1)
    f_z[z] = functools.reduce(jnp.add, [f_y[k] for k in range(NY)])
    for _, device in zs:
        send(f_z.at[z], f_z.at[z], 2, device)
    for i, (t0, nt) in enumerate(CHUNKS):
        cols = pl.ds(t0 * 128, nt * 128)
        arrive(m_other.at[:, cols], 4 + i)
        for k, piece in enumerate(split3(m_own[:, cols] + m_other[:, cols])):
            pair[pl.ds(ROWS * k, ROWS), cols] = piece
    arrive(f_z.at[pl.ds(0, NZ - 1)], 2)
    half = pl.ds(2 * c, 2)
    f_full[half] = functools.reduce(jnp.add, [f_z[k] for k in range(NZ)])
    send(f_full.at[half], f_full.at[half], 3, other)

    left = jnp.concatenate(split3(f_full[half].reshape(RANK // 2, ROWS)), axis=0)
    left = jnp.concatenate([left, left, left], axis=1)

    def project(i):
        t0, nt = PARTS[i]
        three = jnp.dot(left, pair[:, pl.ds(t0 * 128, nt * 128)], preferred_element_type=F32)
        term = three[:16] + (three[16:32] + three[32:])
        for t in range(nt):
            for r in range(2):
                p_sum[atom_of(t0 + t) + r] = term[8 * r : 8 * r + 8, 128 * t : 128 * t + 128]

    project(1)
    for yy, device in ys:
        send(p_sum.at[pl.ds(ATOMS_B + na * yy, na)], a_one.at[y], 9, device)
    a_one[y] = p_sum[pl.ds(ATOMS_B + na * y, na)]
    project(0)
    for zz, device in zs:
        send(p_sum.at[pl.ds(nb * zz, nb)], b_one.at[z], 8, device)
    b_one[z] = p_sum[pl.ds(nb * z, nb)]

    arrive(f_full.at[pl.ds(0, 2)], 3)
    factor = f_full[...].reshape(RANK, ROWS)
    work[...] = eliminate(start_elimination(dot_f32(factor, factor, ((1,), (1,)))), 0, FIRST_STEPS)
    arrive(a_one.at[pl.ds(0, NY - 1)], 9)
    a_two[z] = functools.reduce(jnp.add, [a_one[k] for k in range(NY)])
    for _, device in zs:
        send(a_two.at[z], a_two.at[z], 10, device)
    arrive(b_one.at[pl.ds(0, NZ - 1)], 8)
    b_two[y] = functools.reduce(jnp.add, [b_one[k] for k in range(NZ)])
    for _, device in ys:
        send(b_two.at[y], b_two.at[y], 11, device)

    arrive(b_two.at[pl.ds(0, NY - 1)], 11)
    own_b = pl.ds(nb * z, nb)
    fin[c, own_b] = functools.reduce(jnp.add, [b_two[k] for k in range(NY)])
    for _, device in zs:
        send(fin.at[c, own_b], fin.at[c, own_b], 13, device)
    arrive(a_two.at[pl.ds(0, NZ - 1)], 10)
    own_a = pl.ds(ATOMS_B + na * y, na)
    fin[c, own_a] = functools.reduce(jnp.add, [a_two[k] for k in range(NZ)])
    for _, device in ys:
        send(fin.at[c, own_a], fin.at[c, own_a], 14, device)

    inverse = eliminate(work[...], FIRST_STEPS, RANK)[:, RANK : 2 * RANK]
    ortho_t = dot_f32(inverse, factor, ((1,), (0,)))
    ortho_ref[...] = ortho_t
    weights = jnp.concatenate([inverse, dot_f32(jnp.swapaxes(ortho_t, 0, 1), inverse, ((1,), (0,)))], axis=0)
    hi, mid, lo = split3(weights * (1.0 / REPLICAS))
    left_ref[...] = jnp.concatenate([hi, hi, hi, mid, mid, lo], axis=1)

    finish()
    part_a, part_b = pl.ds(ATOMS_B, ATOMS_A), pl.ds(0, ATOMS_B)
    arrive(fin.at[c, pl.ds(0, ATOMS_A - na)], 14)
    send(fin.at[c, part_a], fin.at[c, part_a], 15, other)
    arrive(fin.at[c, pl.ds(0, ATOMS_B - nb)], 13)
    send(fin.at[c, part_b], fin.at[c, part_b], 16, other)
    arrive(fin.at[c, part_a], 15)
    arrive(fin.at[c, part_b], 16)
    finish()


def apply_kernel(ge, total, ortho, left, ortho_ref, q_ref, error_ref, qv, err, out_sem):
    ortho_ref[...] = ortho[...]
    outs = []
    for i, (t0, nt) in enumerate(CHUNKS):
        cols = pl.ds(t0 * 128, nt * 128)
        rows = [jnp.concatenate([total[r // 2, atom_of(t0 + t) + r % 2] for t in range(nt)], axis=1) for r in range(4)]
        both = jnp.dot(left[...], stack_right(jnp.concatenate(rows, axis=0)), preferred_element_type=F32)
        qv[:, cols] = both[:RANK]
        merged = ge[pl.ds(0, ROWS), cols].astype(F32) + ge[pl.ds(ROWS, ROWS), cols].astype(F32)
        err[:, cols] = (merged - both[RANK:]).astype(BF16)
        group = [
            pltpu.make_async_copy(qv.at[:, cols], q_ref.at[:, cols], out_sem.at[2 * i]),
            pltpu.make_async_copy(err.at[:, cols], error_ref.at[0, :, cols], out_sem.at[2 * i + 1]),
        ]
        for copy in group:
            copy.start()
        outs += group
    for copy in outs:
        copy.wait()


def stack_right(v):
    hi, mid, lo = split3(v)
    return jnp.concatenate([hi, mid, lo, hi, mid, hi], axis=0)


def atoms(*lead):
    return pltpu.VMEM((*lead, 8, 128), F32)


VMEM, HBM = pl.BlockSpec(memory_space=pltpu.VMEM), pl.BlockSpec(memory_space=pltpu.HBM)


def reduce_all(grads, error, q_t):
    na, nb = ATOMS_A // NY, ATOMS_B // NZ
    return pl.pallas_call(
        reduce_kernel,
        out_shape=(
            jax.ShapeDtypeStruct((2 * ROWS, LOCAL), BF16),
            jax.ShapeDtypeStruct((2, ATOMS, 8, 128), F32),
            jax.ShapeDtypeStruct((RANK, ROWS), F32),
            jax.ShapeDtypeStruct((RANK + ROWS, 6 * RANK), BF16),
        ),
        in_specs=[HBM] * 3,
        out_specs=(VMEM,) * 4,
        scratch_shapes=[
            pltpu.VMEM((RANK, LOCAL), F32),
            pltpu.VMEM((RANK, 128), F32),
            atoms(4), atoms(2 * NX, 2), atoms(NY, 2), atoms(NZ, 2), atoms(4),
            pltpu.VMEM((ROWS, LOCAL), F32), pltpu.VMEM((ROWS, LOCAL), F32), pltpu.VMEM((3 * ROWS, LOCAL), BF16), atoms(ATOMS),
            atoms(NY, na), atoms(NZ, nb), atoms(NZ, na), atoms(NY, nb),
            pltpu.SemaphoreType.DMA((3 * len(PARTS),)),
            pltpu.SemaphoreType.DMA((17,)),
            pltpu.SemaphoreType.DMA((17,)),
        ],
        compiler_params=pltpu.CompilerParams(collective_id=0, has_side_effects=True, vmem_limit_bytes=32 * 2**20),
        name="reduce_factors",
    )(*[pltpu.with_memory_space_constraint(v, pltpu.HBM) for v in (grads, error, q_t)])


def apply_all(ge, total, ortho_t, left):
    return pl.pallas_call(
        apply_kernel,
        out_shape=(
            jax.ShapeDtypeStruct((RANK, ROWS), F32),
            jax.ShapeDtypeStruct((RANK, LOCAL), F32),
            jax.ShapeDtypeStruct((1, ROWS, LOCAL), BF16),
        ),
        in_specs=[VMEM] * 4,
        out_specs=(VMEM, HBM, HBM),
        scratch_shapes=[
            pltpu.VMEM((RANK, LOCAL), F32),
            pltpu.VMEM((ROWS, LOCAL), BF16),
            pltpu.SemaphoreType.DMA((2 * len(CHUNKS),)),
        ],
        compiler_params=pltpu.CompilerParams(vmem_limit_bytes=20 * 2**20),
        name="apply_factors",
    )(ge, total, ortho_t, left)


def shards(grads, error, q_prev):
    ortho_t, q_t, error_next = apply_all(*reduce_all(grads, error, jnp.swapaxes(q_prev, 0, 1)))
    return jnp.swapaxes(ortho_t, 0, 1), jnp.swapaxes(q_t, 0, 1), error_next


def solution(mesh):
    in_specs = (P("rep", None, "tp"), P("rep", None, "tp"), P("tp", None))
    out_specs = (P(), P("tp", None), P("rep", None, "tp"))
    return jax.shard_map(shards, mesh=mesh, in_specs=in_specs, out_specs=out_specs, check_vma=False)
```

```python
import functools

import jax
import jax.numpy as jnp
from jax import lax
from jax.experimental import pallas as pl
from jax.experimental.pallas import tpu as pltpu
from jax.sharding import PartitionSpec as P

NZ, NY, NX = 12, 8, 4
ROWS, RANK = 128, 32
REPLICAS = 192
LOCAL = 5504
TILES = LOCAL // 128
ATOMS_A, ATOMS_B = 40, 48
TILES_B = 23
ATOMS = ATOMS_A + ATOMS_B
CHUNKS = ((0, 12), (12, 11), (23, 10), (33, 10))
PARTS = ((0, 23), (23, 20))
FIRST_STEPS = 20
MESH = pl.DeviceIdType.MESH
F32, BF16 = jnp.float32, jnp.bfloat16


def split3(v):
    hi = v.astype(BF16)
    rest = v - hi.astype(F32)
    mid = rest.astype(BF16)
    lo = (rest - mid.astype(F32)).astype(BF16)
    return hi, mid, lo


def atom_of(tile):
    return 2 * tile if tile < TILES_B else ATOMS_B + 2 * (tile - TILES_B)


def far_first(n):
    return sorted(range(1, n), key=lambda k: (-min(k, n - k), k))


def drain(ref, sem):
    pltpu.make_async_copy(ref, ref, sem).wait()


def dot_f32(a, b, dims):
    return lax.dot_general(a, b, (dims, ((), ())), precision=lax.Precision.HIGHEST, preferred_element_type=F32)


def start_elimination(gram):
    row = lax.broadcasted_iota(jnp.int32, (RANK, 128), 0)
    lane = lax.broadcasted_iota(jnp.int32, (RANK, 128), 1)
    work = jnp.concatenate([gram, jnp.zeros((RANK, 128 - RANK), F32)], axis=1)
    return work + (lane == row + RANK).astype(F32)


def eliminate(work, begin, end):
    row = lax.broadcasted_iota(jnp.int32, (RANK, 128), 0)
    lane = lax.broadcasted_iota(jnp.int32, (RANK, 128), 1)

    def step(k, work):
        column = jnp.sum(jnp.where(lane == k, work, 0.0), axis=1, keepdims=True)
        at_row = jnp.sum(jnp.where(row == k, work, 0.0), axis=0, keepdims=True)
        pivot = jnp.sum(jnp.where(row[:, :1] == k, column, 0.0), axis=0, keepdims=True)
        scale = lax.rsqrt(pivot)
        scale = scale * (1.5 - 0.5 * (pivot * scale) * scale)
        scaled = at_row * scale
        reduced = work - jnp.where(row[:, :1] > k, column * scale, 0.0) * scaled
        return jnp.where(row == k, scaled, reduced)

    return lax.fori_loop(begin, end, step, work)


def reduce_kernel(
    g_ref, e_ref, q_ref, ge, fin, ortho_ref, left_ref,
    qv, work, f_part, f_cx, f_y, f_z, f_full, m_own, m_other, pair, p_sum, a_one, b_one, a_sum, a_two, b_two,
    load_sem, ssem, rsem,
):
    rep, x = lax.axis_index("rep"), lax.axis_index("tp")
    c = lax.rem(rep, 2)
    y = lax.rem(rep // 2, NY)
    z = rep // (2 * NY)
    na, nb = ATOMS_A // NY, ATOMS_B // NZ

    def at(zz, yy, cc, xx):
        return {"rep": (zz * NY + yy) * 2 + cc, "tp": xx}

    other = at(z, y, 1 - c, x)
    xs = [(k, lax.rem(x + k, NX)) for k in far_first(NX)]
    cxs = [(lax.rem(c + flip, 2), at(z, y, lax.rem(c + flip, 2), xx)) for flip in (1, 0) for _, xx in xs]
    cxs.append((1 - c, other))
    ys = [(yy, at(z, yy, c, x)) for yy in [lax.rem(y + k, NY) for k in far_first(NY)]]
    zs = [(zz, at(zz, y, c, x)) for zz in [lax.rem(z + k, NZ) for k in far_first(NZ)]]
    sent = []

    def send(src, dst, sem, device):
        pltpu.make_async_remote_copy(
            src_ref=src, dst_ref=dst, send_sem=ssem.at[sem], recv_sem=rsem.at[sem], device_id=device, device_id_type=MESH
        ).start()

    def arrive(ref, sem):
        drain(ref, rsem.at[sem])
        sent.append((ref, sem))

    def finish():
        while sent:
            ref, sem = sent.pop(0)
            drain(ref, ssem.at[sem])

    barrier = pltpu.get_barrier_semaphore()
    partners = [d for _, d in zs] + [d for _, d in ys] + [d for _, d in cxs]
    for device in partners:
        pl.semaphore_signal(barrier, inc=1, device_id=device, device_id_type=MESH)

    loads = []
    for i, (t0, nt) in enumerate(PARTS):
        cols = pl.ds(t0 * 128, nt * 128)
        group = [
            pltpu.make_async_copy(q_ref.at[:, cols], qv.at[:, cols], load_sem.at[3 * i]),
            pltpu.make_async_copy(g_ref.at[0, :, cols], ge.at[pl.ds(0, ROWS), cols], load_sem.at[3 * i + 1]),
            pltpu.make_async_copy(e_ref.at[0, :, cols], ge.at[pl.ds(ROWS, ROWS), cols], load_sem.at[3 * i + 2]),
        ]
        for copy in group:
            copy.start()
        loads.append(group)

    both = jnp.zeros((3 * RANK, 2 * ROWS), F32)
    for (t0, nt), group in zip(PARTS, loads, strict=True):
        for copy in group:
            copy.wait()
        cols = pl.ds(t0 * 128, nt * 128)
        left = jnp.concatenate(split3(qv[:, cols]), axis=0)
        both += lax.dot_general(left, ge[:, cols], (((1,), (1,)), ((), ())), preferred_element_type=F32)
    both = both[:, :ROWS] + both[:, ROWS:]
    part = both[:RANK] + (both[RANK : 2 * RANK] + both[2 * RANK :])
    f_part[...] = part.reshape(4, 8, 128)
    pad = pl.ds(2 * TILES_B, ATOMS_B - 2 * TILES_B)
    p_sum[pad] = jnp.zeros((ATOMS_B - 2 * TILES_B, 8, 128), F32)
    pl.semaphore_wait(barrier, len(partners))

    own = 2 * x + c
    for cc, device in cxs:
        send(f_part.at[pl.ds(2 * cc, 2)], f_cx.at[own], 0, device)
    f_cx[own] = f_part[pl.ds(2 * c, 2)]
    for t0, nt in CHUNKS:
        cols = pl.ds(t0 * 128, nt * 128)
        m_own[:, cols] = ge[pl.ds(0, ROWS), cols].astype(F32) + ge[pl.ds(ROWS, ROWS), cols].astype(F32)
    arrive(f_cx.at[pl.ds(0, 2 * NX - 1)], 0)
    f_y[y] = functools.reduce(jnp.add, [f_cx[k] for k in range(2 * NX)])
    for _, device in ys:
        send(f_y.at[y], f_y.at[y], 1, device)
    for i, (t0, nt) in enumerate(CHUNKS):
        cols = pl.ds(t0 * 128, nt * 128)
        send(m_own.at[:, cols], m_other.at[:, cols], 4 + i, other)
    arrive(f_y.at[pl.ds(0, NY - 1)], 1)
    f_z[z] = functools.reduce(jnp.add, [f_y[k] for k in range(NY)])
    for _, device in zs:
        send(f_z.at[z], f_z.at[z], 2, device)
    for i, (t0, nt) in enumerate(CHUNKS):
        cols = pl.ds(t0 * 128, nt * 128)
        arrive(m_other.at[:, cols], 4 + i)
        for k, piece in enumerate(split3(m_own[:, cols] + m_other[:, cols])):
            pair[pl.ds(ROWS * k, ROWS), cols] = piece
    arrive(f_z.at[pl.ds(0, NZ - 1)], 2)
    half = pl.ds(2 * c, 2)
    f_full[half] = functools.reduce(jnp.add, [f_z[k] for k in range(NZ)])
    send(f_full.at[half], f_full.at[half], 3, other)

    left = jnp.concatenate(split3(f_full[half].reshape(RANK // 2, ROWS)), axis=0)
    left = jnp.concatenate([left, left, left], axis=1)

    def project(i):
        t0, nt = PARTS[i]
        three = jnp.dot(left, pair[:, pl.ds(t0 * 128, nt * 128)], preferred_element_type=F32)
        term = three[:16] + (three[16:32] + three[32:])
        for t in range(nt):
            for r in range(2):
                p_sum[atom_of(t0 + t) + r] = term[8 * r : 8 * r + 8, 128 * t : 128 * t + 128]

    project(1)
    for yy, device in ys:
        send(p_sum.at[pl.ds(ATOMS_B + na * yy, na)], a_one.at[y], 9, device)
    a_one[y] = p_sum[pl.ds(ATOMS_B + na * y, na)]
    project(0)
    for zz, device in zs:
        send(p_sum.at[pl.ds(nb * zz, nb)], b_one.at[z], 8, device)
    b_one[z] = p_sum[pl.ds(nb * z, nb)]

    arrive(f_full.at[pl.ds(0, 2)], 3)
    factor = f_full[...].reshape(RANK, ROWS)
    work[...] = eliminate(start_elimination(dot_f32(factor, factor, ((1,), (1,)))), 0, FIRST_STEPS)
    owners = [NZ * j // na for j in range(na)]
    owned = [z == zz for zz in owners]
    is_owner = functools.reduce(jnp.logical_or, owned)
    arrive(a_one.at[pl.ds(0, NY - 1)], 9)
    a_sum[...] = functools.reduce(jnp.add, [a_one[k] for k in range(NY)])
    for j, zz in enumerate(owners):

        @pl.when(z != zz)
        def _(j=j, zz=zz):
            send(a_sum.at[j], a_two.at[z], 10, at(zz, y, c, x))

        @pl.when(z == zz)
        def _(j=j):
            a_two[z] = a_sum[j]

    arrive(b_one.at[pl.ds(0, NZ - 1)], 8)
    b_two[y] = functools.reduce(jnp.add, [b_one[k] for k in range(NZ)])
    for _, device in ys:
        send(b_two.at[y], b_two.at[y], 11, device)

    for j in range(na):

        @pl.when(owned[j])
        def _(j=j):
            drain(a_two.at[pl.ds(0, NZ - 1)], rsem.at[10])
            mine = ATOMS_B + na * y + j
            fin[c, mine] = functools.reduce(jnp.add, [a_two[k] for k in range(NZ)])
            for _, device in zs:
                send(fin.at[c, mine], fin.at[c, mine], 12, device)

    arrive(b_two.at[pl.ds(0, NY - 1)], 11)
    own_b = pl.ds(nb * z, nb)
    fin[c, own_b] = functools.reduce(jnp.add, [b_two[k] for k in range(NY)])
    for _, device in zs:
        send(fin.at[c, own_b], fin.at[c, own_b], 13, device)

    @pl.when(is_owner)
    def _():
        drain(a_sum.at[pl.ds(0, na - 1)], rsem.at[12])

    @pl.when(jnp.logical_not(is_owner))
    def _():
        drain(a_sum, rsem.at[12])

    own_a = pl.ds(ATOMS_B + na * y, na)
    for _, device in ys:
        send(fin.at[c, own_a], fin.at[c, own_a], 14, device)

    inverse = eliminate(work[...], FIRST_STEPS, RANK)[:, RANK : 2 * RANK]
    ortho_t = dot_f32(inverse, factor, ((1,), (0,)))
    ortho_ref[...] = ortho_t
    weights = jnp.concatenate([inverse, dot_f32(jnp.swapaxes(ortho_t, 0, 1), inverse, ((1,), (0,)))], axis=0)
    hi, mid, lo = split3(weights * (1.0 / REPLICAS))
    left_ref[...] = jnp.concatenate([hi, hi, hi, mid, mid, lo], axis=1)

    @pl.when(is_owner)
    def _():
        drain(a_sum.at[pl.ds(0, na - 1)], ssem.at[10])
        drain(a_two.at[pl.ds(0, NZ - 1)], ssem.at[12])

    @pl.when(jnp.logical_not(is_owner))
    def _():
        drain(a_sum, ssem.at[10])

    finish()
    part_a, part_b = pl.ds(ATOMS_B, ATOMS_A), pl.ds(0, ATOMS_B)
    arrive(fin.at[c, pl.ds(0, ATOMS_B - nb)], 13)
    send(fin.at[c, part_b], fin.at[c, part_b], 16, other)
    arrive(fin.at[c, pl.ds(0, ATOMS_A - na)], 14)
    send(fin.at[c, part_a], fin.at[c, part_a], 15, other)
    arrive(fin.at[c, part_b], 16)
    arrive(fin.at[c, part_a], 15)
    finish()


def apply_kernel(ge, total, ortho, left, ortho_ref, q_ref, error_ref, qv, err, out_sem):
    ortho_ref[...] = ortho[...]
    outs = []
    for i, (t0, nt) in enumerate(CHUNKS):
        cols = pl.ds(t0 * 128, nt * 128)
        rows = [jnp.concatenate([total[r // 2, atom_of(t0 + t) + r % 2] for t in range(nt)], axis=1) for r in range(4)]
        both = jnp.dot(left[...], stack_right(jnp.concatenate(rows, axis=0)), preferred_element_type=F32)
        qv[:, cols] = both[:RANK]
        merged = ge[pl.ds(0, ROWS), cols].astype(F32) + ge[pl.ds(ROWS, ROWS), cols].astype(F32)
        err[:, cols] = (merged - both[RANK:]).astype(BF16)
        group = [
            pltpu.make_async_copy(qv.at[:, cols], q_ref.at[:, cols], out_sem.at[2 * i]),
            pltpu.make_async_copy(err.at[:, cols], error_ref.at[0, :, cols], out_sem.at[2 * i + 1]),
        ]
        for copy in group:
            copy.start()
        outs += group
    for copy in outs:
        copy.wait()


def stack_right(v):
    hi, mid, lo = split3(v)
    return jnp.concatenate([hi, mid, lo, hi, mid, hi], axis=0)


def atoms(*lead):
    return pltpu.VMEM((*lead, 8, 128), F32)


VMEM, HBM = pl.BlockSpec(memory_space=pltpu.VMEM), pl.BlockSpec(memory_space=pltpu.HBM)


def reduce_all(grads, error, q_t):
    na, nb = ATOMS_A // NY, ATOMS_B // NZ
    return pl.pallas_call(
        reduce_kernel,
        out_shape=(
            jax.ShapeDtypeStruct((2 * ROWS, LOCAL), BF16),
            jax.ShapeDtypeStruct((2, ATOMS, 8, 128), F32),
            jax.ShapeDtypeStruct((RANK, ROWS), F32),
            jax.ShapeDtypeStruct((RANK + ROWS, 6 * RANK), BF16),
        ),
        in_specs=[HBM] * 3,
        out_specs=(VMEM,) * 4,
        scratch_shapes=[
            pltpu.VMEM((RANK, LOCAL), F32),
            pltpu.VMEM((RANK, 128), F32),
            atoms(4), atoms(2 * NX, 2), atoms(NY, 2), atoms(NZ, 2), atoms(4),
            pltpu.VMEM((ROWS, LOCAL), F32), pltpu.VMEM((ROWS, LOCAL), F32), pltpu.VMEM((3 * ROWS, LOCAL), BF16), atoms(ATOMS),
            atoms(NY, na), atoms(NZ, nb), atoms(na), atoms(NZ), atoms(NY, nb),
            pltpu.SemaphoreType.DMA((3 * len(PARTS),)),
            pltpu.SemaphoreType.DMA((17,)),
            pltpu.SemaphoreType.DMA((17,)),
        ],
        compiler_params=pltpu.CompilerParams(collective_id=0, has_side_effects=True, vmem_limit_bytes=32 * 2**20),
        name="reduce_factors",
    )(*[pltpu.with_memory_space_constraint(v, pltpu.HBM) for v in (grads, error, q_t)])


def apply_all(ge, total, ortho_t, left):
    return pl.pallas_call(
        apply_kernel,
        out_shape=(
            jax.ShapeDtypeStruct((RANK, ROWS), F32),
            jax.ShapeDtypeStruct((RANK, LOCAL), F32),
            jax.ShapeDtypeStruct((1, ROWS, LOCAL), BF16),
        ),
        in_specs=[VMEM] * 4,
        out_specs=(VMEM, HBM, HBM),
        scratch_shapes=[
            pltpu.VMEM((RANK, LOCAL), F32),
            pltpu.VMEM((ROWS, LOCAL), BF16),
            pltpu.SemaphoreType.DMA((2 * len(CHUNKS),)),
        ],
        compiler_params=pltpu.CompilerParams(vmem_limit_bytes=20 * 2**20),
        name="apply_factors",
    )(ge, total, ortho_t, left)


def shards(grads, error, q_prev):
    ortho_t, q_t, error_next = apply_all(*reduce_all(grads, error, jnp.swapaxes(q_prev, 0, 1)))
    return jnp.swapaxes(ortho_t, 0, 1), jnp.swapaxes(q_t, 0, 1), error_next


def solution(mesh):
    in_specs = (P("rep", None, "tp"), P("rep", None, "tp"), P("tp", None))
    out_specs = (P(), P("tp", None), P("rep", None, "tp"))
    return jax.shard_map(shards, mesh=mesh, in_specs=in_specs, out_specs=out_specs, check_vma=False)
```
